32 devices in a mesh: groups: 2 (over y), expert: 4 (over z), dp: 2 (over x), sub: 2 (over core).
Axes of the slice: x: 2, y: 2, z: 4, core: 2. Of those that a mesh axis runs over, the one named last changes fastest.
Arguments:
- tokens: bfloat16 [384, 4096], P(('groups', 'expert', 'dp', 'sub')), parts along dimension 0, may hold values from -6 to 6
- cotangent: bfloat16 [384, 4096], P(('groups', 'expert', 'dp', 'sub')), parts along dimension 0, may hold values from -1.5 to 1.5
- routes: int32 [384, 2], P(('groups', 'expert', 'dp', 'sub')), parts along dimension 0, may hold values from 0 to 3, all different within a row; in each aligned block of 12 rows (0 to 11, 12 to 23, ...) at most 12 rows name the same one
- probs: bfloat16 [384, 2], P(('groups', 'expert', 'dp', 'sub')), parts along dimension 0, may hold values from 0.19921875 to 1
- gate_weight: bfloat16 [4, 1536, 4096], P('expert', ('dp', 'sub')), may hold values from -0.09375 to 0.09375
- up_weight: bfloat16 [4, 1536, 4096], P('expert', ('dp', 'sub')), may hold values from -0.09375 to 0.09375
- down_weight: bfloat16 [4, 1536, 4096], P('expert', ('dp', 'sub')), may hold values from -0.09375 to 0.09375
- keep: int32 [4, 1536], P('expert'), may hold values 0 or 1
Outputs:
- fisher: float32 [8, 1536, 1536], P(('groups', 'expert'), ('dp', 'sub')), parts along dimension 0
- masks: float32 [8, 1536], P(('groups', 'expert'), ('dp', 'sub')), parts along dimension 0
- token_scores: float32 [384, 2], P(('groups', 'expert', 'dp', 'sub')), parts along dimension 0
The draws below stay inside these ranges and needn't reach their ends.
There are 2 independent parts, one for each index of `groups`. The reference program is written for one: setup_inputs(seed, part) draws one part's arguments, and reference() takes and returns one part's arrays. A program takes and returns all parts, laid end to end along the dimension named above; an argument that names none is the same for every part. Nothing has to cross between parts.
Inputs may be any that keep to these rules, and one draw needn't show every extreme that they name: `routes`: the 2 experts of a token differ. Among the tokens of one device (aligned blocks of 12 rows) no expert is named more than 12 times, a bound that some block reaches.
All inputs are finite; a program needn't handle non-finite values. No bound on the sum of `keep` on one device may be relied on, other than what follows from the above.
Results may differ from the reference program's by a relative error of at most 0.0041.
Values may be sent and summed in bfloat16 or wider, within the bound.
A program may use at most 64 MiB of HBM per device.

```python
import math
import jax
import jax.numpy as jnp
import numpy as np
from jax import lax

D = 4096
H = 1536
TOK_DEV = 12
TOPK = 2
EXPERTS = 4
CAP = 12
TOKENS = 192


def plant(values, stream_key, smallest, top_value):
    longest = values.shape.index(max(values.shape))
    spots = []
    for shift in (0, 1):
        where = [jax.random.randint(jax.random.fold_in(stream_key, axis), (), 0, length) for axis, length in enumerate(values.shape)]
        where[longest] = (where[longest] + shift) % values.shape[longest]
        spots.append(tuple(where))
    return values.at[spots[0]].set(smallest).at[spots[1]].set(top_value)


def level_of(stream_key, dims, shards, smallest, high):
    factor_of = 1.0
    for axis_at, parts in shards:
        draws = jax.random.uniform(jax.random.fold_in(jax.random.fold_in(stream_key, 6), axis_at), (parts,), jnp.float32, smallest / len(shards), high / len(shards))
        factor_of = factor_of * jnp.repeat(jnp.exp(draws), dims[axis_at] // parts).reshape((-1,) + (1,) * (len(dims) - 1 - axis_at))
    return factor_of


def assign_block(own_key, own, number, rows, amount, top, most, lean):
    order = jax.random.permutation(own_key, amount)
    crowded, common = shares(amount, rows * top, most, lean, True), shares(amount, rows * top, most, lean, False)
    places = jnp.arange(amount)

    def named(tallies, offset_by):
        used = int((tallies > 0).sum())
        fixed = max(1, used // 4)
        shifted = fixed + (places - fixed + offset_by * (used - fixed)) % max(1, amount - fixed)
        return jnp.zeros((amount,), jnp.int32).at[order[jnp.where(places < fixed, places, shifted)]].set(jnp.asarray(tallies, jnp.int32))

    tallies = jnp.where(number % 4 == 0, named(crowded, number // 4), named(common, number - number // 4 - 1))
    mixed = jax.random.permutation(jax.random.fold_in(own, 3), amount)
    donor, receiver = mixed[0:amount // 2 * 2:2], mixed[1:amount // 2 * 2:2]
    margin = jnp.minimum(tallies[donor] - 1, most - tallies[receiver]) // 2
    margin = jnp.where((donor == order[0]) | (receiver == order[0]) | (tallies[receiver] == 0), 0, jnp.maximum(margin, 0))
    shifted = jax.random.randint(jax.random.fold_in(own, 4), (amount // 2,), 0, 1 << 20) % (margin + 1)
    tallies = tallies.at[donor].add(-shifted).at[receiver].add(shifted)
    members = jnp.searchsorted(jnp.cumsum(tallies), jnp.arange(rows * top), side="right").astype(jnp.int32)
    listing = members.reshape(top, rows).T
    listing = listing[jax.random.permutation(jax.random.fold_in(own, 1), rows)]
    offset_by = jax.random.randint(jax.random.fold_in(own, 2), (rows, 1), 0, top)
    return jnp.take_along_axis(listing, (jnp.arange(top)[None, :] + offset_by) % top, axis=1)


def shares(number_of, total, reach, skew, full):
    loads = [(1 << 20) // math.isqrt(rank ** skew) + 1 for rank in range(1, number_of + 1)]
    largest = reach if full else min(reach, max(-(-total // number_of), total * loads[0] // sum(loads)))
    least = 1 if total - largest >= number_of - 1 else 0
    given, rest = [largest] + [least] * (number_of - 1), total - largest - least * (number_of - 1)
    while rest > 0:
        free = [i for i in range(1, number_of) if given[i] < largest] or [i for i in range(1, number_of) if given[i] < reach]
        pool, budget = sum([loads[i] for i in free]), rest
        for i in free:
            more = min(reach - given[i], max(1, budget * loads[i] // pool), rest)
            given[i] = given[i] + more
            rest = rest - more
    return np.array(given)


def normal_values(rng, extent, deviation, most, cuts=(), kind=jnp.bfloat16):
    result = jax.random.normal(rng, extent, jnp.float32) * deviation
    if len(cuts) > 0:
        result = level_of(rng, extent, cuts, -0.22, 0.18) * result
    return jnp.clip(result, min=-most, max=most).astype(kind)


def setup_inputs(seed: int = 0, part: int = 0) -> dict:
    streams_of = jax.random.split(jax.random.key(seed), 9)
    own_keys = jax.random.split(jax.random.fold_in(streams_of[8], part), 9)
    tokens = normal_values(own_keys[0], (TOKENS, D), 1.0, 6.0, ((0, 16),))
    cotangent = normal_values(own_keys[1], (TOKENS, D), 0.25, 1.5, ((0, 16),))
    routes_keys = jax.random.split(jax.random.fold_in(own_keys[2], 1), TOKENS // TOK_DEV)
    routes_turns = jax.random.permutation(jax.random.fold_in(own_keys[2], 3), TOKENS // TOK_DEV)
    routes = jax.vmap(lambda own, number: assign_block(jax.random.fold_in(own_keys[2], 2), own, number, TOK_DEV, EXPERTS, TOPK, CAP, 2))(routes_keys, routes_turns).reshape((TOKENS, TOPK))
    probs = jnp.clip(0.19921875 + 0.80078125 * jax.random.uniform(own_keys[3], (TOKENS, TOPK), jnp.float32) ** level_of(own_keys[3], (TOKENS, TOPK), ((0, 16),), -0.2, 0.2), 0.19921875, 1.0).astype(jnp.bfloat16)
    gate_weight = normal_values(streams_of[4], (EXPERTS, H, D), D ** -0.5, 0.09375, ((0, 4), (1, 4)))
    up_weight = normal_values(streams_of[5], (EXPERTS, H, D), D ** -0.5, 0.09375, ((0, 4), (1, 4)))
    down_weight = normal_values(streams_of[6], (EXPERTS, H, D), D ** -0.5, 0.09375, ((0, 4), (1, 4)))
    keep = plant((jax.random.randint(streams_of[7], (EXPERTS, H), 0, 5) < 3).astype(jnp.int32), jax.random.fold_in(streams_of[7], 1), 0, 1)
    return dict(tokens=tokens, cotangent=cotangent, routes=routes, probs=probs, gate_weight=gate_weight, up_weight=up_weight, down_weight=down_weight, keep=keep)


def reference(tokens, cotangent, routes, probs, gate_weight, up_weight, down_weight, keep):
    sources = TOKENS // TOK_DEV
    pair_count = TOK_DEV * TOPK
    row_total = sources * CAP
    grouped = routes.reshape(sources, pair_count).astype(jnp.int32)
    onehot = (grouped[:, :, None] == jnp.arange(EXPERTS, dtype=jnp.int32)[None, None, :]).astype(jnp.int32)
    before = jnp.cumsum(onehot, axis=1) - onehot
    slot_index = lax.optimization_barrier(jnp.sum(onehot * before, axis=2)).astype(jnp.int32)
    row_index = (jnp.arange(sources, dtype=jnp.int32)[:, None] * CAP + slot_index).astype(jnp.int32)
    token_index = (jnp.arange(sources, dtype=jnp.int32)[:, None] * TOK_DEV + jnp.arange(pair_count, dtype=jnp.int32)[None, :] // TOPK).astype(jnp.int32)
    table = jnp.full((EXPERTS, row_total), TOKENS, jnp.int32).at[grouped, row_index].set(token_index)
    prob_table = jnp.zeros((EXPERTS, row_total), jnp.float32).at[grouped, row_index].set(probs.astype(jnp.float32).reshape(sources, pair_count))
    padded_tok = jnp.concatenate([tokens, jnp.zeros((1, D), tokens.dtype)], axis=0)
    padded_cot = jnp.concatenate([cotangent, jnp.zeros((1, D), cotangent.dtype)], axis=0)

    def per_expert(inputs):
        indices, row_probs, w_gate, w_up, w_down, kept = inputs
        rows_tok = padded_tok[indices]
        rows_cot = padded_cot[indices]
        gate_pre = jnp.dot(rows_tok, w_gate.T, preferred_element_type=jnp.float32)
        up_pre = jnp.dot(rows_tok, w_up.T, preferred_element_type=jnp.float32)
        back_pre = jnp.dot(rows_cot, w_down.T, preferred_element_type=jnp.float32)
        grads = (row_probs[:, None] * (jax.nn.silu(gate_pre) * up_pre) * back_pre).astype(jnp.bfloat16)
        fisher = jnp.dot(grads.T, grads, preferred_element_type=jnp.float32)
        totals = lax.optimization_barrier(jnp.sum(jnp.square(grads.astype(jnp.float32)), axis=1))
        kept_units = kept.astype(jnp.float32)
        pull = jnp.dot(fisher, 1.0 - kept_units, precision=lax.Precision.HIGHEST)
        masks = kept_units * (1.0 + pull / (jnp.diagonal(fisher) + 1e-05))
        return (fisher, masks, totals)
    fisher, masks, totals = lax.map(per_expert, (table, prob_table, gate_weight, up_weight, down_weight, keep))
    pair_totals = totals[grouped, row_index]
    token_scores = jnp.sqrt(pair_totals + 1e-05).reshape(TOKENS, TOPK)
    return (fisher, masks, token_scores)
```

```python
import functools

import jax
import jax.numpy as jnp
from jax import lax
from jax.experimental import pallas as pl
from jax.experimental.pallas import tpu as pltpu
from jax.sharding import PartitionSpec as P

MESH = pl.DeviceIdType.MESH
SLOT = 16
LANES = 128


def pack(values, front):
    rows, width = values.shape
    quarter = width // 4
    last = values[:, 3 * quarter:]
    folded = [last[4 * j:4 * j + 4] for j in range(3)] + [jnp.zeros((4, quarter), values.dtype)]
    lower = jnp.concatenate([jnp.zeros((4, LANES), values.dtype)] * (front is not None) + folded, axis=1)
    upper = values if front is None else jnp.concatenate([front, values], axis=1)
    return jnp.concatenate([upper, lower], axis=0)


def fused(
    tokens, cotangent, routes, probs, w_gate, w_up, w_down, keep,
    fisher, masks, scores,
    tok, cot, wgu, wd, pre, back, grads, totals, returned,
    load_sem, tok_send, tok_recv, cot_send, cot_recv, grad_send, grad_recv, tot_send, tot_recv,
    *, planes,
):
    z, x, s = lax.axis_index("expert"), lax.axis_index("dp"), lax.axis_index("sub")
    units = w_down.shape[1]
    width = tokens.shape[1]
    quarter = width // 4
    count = planes * 4

    loads = [
        pltpu.make_async_copy(w_gate.at[0], wgu.at[pl.ds(0, units)], load_sem.at[0]),
        pltpu.make_async_copy(w_up.at[0], wgu.at[pl.ds(units, units)], load_sem.at[1]),
        pltpu.make_async_copy(w_down.at[0], wd, load_sem.at[2]),
    ]
    for load in loads:
        load.start()

    barrier = pltpu.get_barrier_semaphore()
    others = [lax.rem(z + k, planes) for k in range(1, planes)]
    across = 1 - x
    twin = 1 - s
    for other in others:
        pl.semaphore_signal(barrier, inc=1, device_id={"expert": other}, device_id_type=MESH)
    pl.semaphore_signal(barrier, inc=1, device_id={"dp": across}, device_id_type=MESH)
    pl.semaphore_signal(barrier, inc=1, device_id={"sub": twin}, device_id_type=MESH)

    def slot(plane, column, core):
        return (plane * 2 + column) * 2 + core

    mine = slot(z, x, s)
    picked = routes[...]
    lane = lax.broadcasted_iota(jnp.int32, (picked.shape[0], LANES), 1)
    weight = probs[...].astype(jnp.float32)
    front = jnp.zeros(lane.shape, jnp.float32)
    for k in range(picked.shape[1]):
        front = front + jnp.where(lane == picked[:, k:k + 1], weight[:, k:k + 1], 0.0)
    tok[mine] = pack(tokens[...].astype(jnp.float32), front).astype(jnp.bfloat16)
    cot[mine] = pack(cotangent[...].astype(jnp.float32), None).astype(jnp.bfloat16)

    pl.semaphore_wait(barrier, planes + 1)

    def sender(buffer, sent, send_sem, recv_sem):
        def copy(index, number, target):
            part = buffer.at[index, :, pl.ds(0, sent)]
            return pltpu.make_async_remote_copy(
                src_ref=part, dst_ref=part, send_sem=send_sem.at[number], recv_sem=recv_sem.at[index],
                device_id=target, device_id_type=MESH,
            )
        return copy

    tok_copy = sender(tok, LANES + 3 * quarter, tok_send, tok_recv)
    cot_copy = sender(cot, 3 * quarter, cot_send, cot_recv)
    pending = []

    def start(copy, index, number, target):
        one = copy(index, number, target)
        one.start()
        pending.append(one)

    def begin(copy):
        start(copy, mine, 0, {"dp": across})
        for k, other in enumerate(others):
            start(copy, mine, 1 + k, {"expert": other})
        start(copy, mine, planes, {"sub": twin})

    def arrive(copy, index):
        copy(index, 0, {"sub": twin}).wait_recv()

    def relay(copy):
        number = planes + 1
        for k in range(planes):
            if k > 0:
                index = slot(others[planes - 1 - k], x, s)
                arrive(copy, index)
                start(copy, index, number, {"dp": across})
                start(copy, index, number + 1, {"sub": twin})
                number += 2
        for k in range(planes):
            index = slot(z if k == 0 else others[planes - 1 - k], across, s)
            arrive(copy, index)
            start(copy, index, number, {"sub": twin})
            number += 1

    def finish(copy):
        for plane in [z] + others[::-1]:
            arrive(copy, slot(plane, x, twin))
            arrive(copy, slot(plane, across, twin))

    def unfold(buffer, base):
        @pl.loop(0, count)
        def _(index):
            folded = buffer[index, :, pl.ds(base, 3 * quarter)].astype(jnp.float32)[12:16]
            pieces = [folded[:, j * quarter:(j + 1) * quarter] for j in range(3)]
            whole = jnp.concatenate(pieces + [jnp.zeros((4, quarter), jnp.float32)], axis=0)
            buffer[index, :, pl.ds(base + 3 * quarter, quarter)] = whole.astype(jnp.bfloat16)

    dims = (((1,), (1,)), ((), ()))
    begin(tok_copy)
    begin(cot_copy)
    relay(tok_copy)
    finish(tok_copy)
    relay(cot_copy)
    unfold(tok, LANES)
    loads[0].wait()
    loads[1].wait()
    step = 2 * units // 3

    @pl.loop(0, 3)
    def _(part):
        rows = pl.ds(pl.multiple_of(part * step, step), step)
        left = tok[:, :, pl.ds(LANES, width)].reshape(count * SLOT, width)
        pre[part] = lax.dot_general(left, wgu[rows], dims, preferred_element_type=jnp.float32)

    loads[2].wait()
    finish(cot_copy)
    unfold(cot, 0)

    back[...] = lax.dot_general(
        cot[...].reshape(count * SLOT, width), wd[...], dims, preferred_element_type=jnp.float32
    )
    both = jnp.concatenate([pre[0], pre[1], pre[2]], axis=1)
    gate, up = both[:, :units], both[:, units:]
    front_all = tok[:, :, pl.ds(0, LANES)].reshape(count * SLOT, LANES).astype(jnp.float32)
    lane_all = lax.broadcasted_iota(jnp.int32, front_all.shape, 1)
    scale = jnp.sum(jnp.where(lane_all == z, front_all, 0.0), axis=1, keepdims=True)
    row = lax.rem(lax.broadcasted_iota(jnp.int32, scale.shape, 0), SLOT)
    scale = jnp.where(row < 12, scale, 0.0)
    silu = gate / (1.0 + jnp.exp(-gate))
    value = scale * (silu * up) * back[...]
    own = x * 2 + s
    compact = jnp.concatenate([value[SLOT * i:SLOT * i + 12] for i in range(count)], axis=0)
    grads[own] = compact.astype(jnp.bfloat16)

    def grad_copy(index, number, target):
        return pltpu.make_async_remote_copy(
            src_ref=grads.at[index], dst_ref=grads.at[index], send_sem=grad_send.at[number],
            recv_sem=grad_recv.at[index], device_id=target, device_id_type=MESH,
        )

    start(grad_copy, own, 0, {"dp": across})
    start(grad_copy, own, 1, {"sub": twin})
    far = across * 2 + s
    arrive(grad_copy, far)
    start(grad_copy, far, 2, {"sub": twin})
    arrive(grad_copy, x * 2 + twin)
    arrive(grad_copy, across * 2 + twin)

    kept = keep[...].astype(jnp.float32)
    square = jnp.zeros((count * 12, LANES), jnp.float32)
    pulled = jnp.zeros((count * 12, LANES), jnp.float32)
    for part in range(4):
        for tile in range(units // LANES):
            piece = grads[part, :, pl.ds(tile * LANES, LANES)].astype(jnp.float32)
            first = part * units + tile * LANES
            square = square + piece * piece
            pulled = pulled + piece * (1.0 - kept[:, first:first + LANES])
    for index in range(count):
        totals[index] = jnp.concatenate(
            [square[12 * index:12 * index + 12], jnp.zeros((4, LANES), jnp.float32)], axis=0
        )

    def total_copy(plane, number, target):
        return pltpu.make_async_remote_copy(
            src_ref=totals.at[slot(plane, x, s)], dst_ref=returned.at[z], send_sem=tot_send.at[number],
            recv_sem=tot_recv.at[z], device_id=target, device_id_type=MESH,
        )

    for k, other in enumerate(others):
        start(total_copy, other, k, {"expert": other})
    returned[z] = totals[mine]

    ours = grads[own]
    for part in range(4):
        fisher[0, :, pl.ds(part * units, units)] = lax.dot_general(
            ours, grads[part], (((0,), (0,)), ((), ())), preferred_element_type=jnp.float32
        )
    wide = ours.astype(jnp.float32)
    pull = jnp.sum(wide * jnp.sum(pulled, axis=1, keepdims=True), axis=0, keepdims=True)
    diagonal = jnp.sum(wide * wide, axis=0, keepdims=True)
    kept_mine = jnp.zeros((1, units), jnp.float32)
    for part in range(4):
        kept_mine = kept_mine + jnp.where(own == part, kept[:, part * units:(part + 1) * units], 0.0)
    masks[...] = kept_mine * (1.0 + pull / (diagonal + 1e-05))

    for other in others:
        pltpu.make_async_remote_copy(
            src_ref=totals.at[mine], dst_ref=returned.at[other], send_sem=tot_send.at[0],
            recv_sem=tot_recv.at[other], device_id={"expert": other}, device_id_type=MESH,
        ).wait_recv()
    result = jnp.zeros((12, picked.shape[1]), jnp.float32)
    choice = routes[...]
    for plane in range(planes):
        total = jnp.sum(returned[plane], axis=1, keepdims=True)[:12]
        result = result + jnp.where(choice == plane, total, 0.0)
    scores[...] = jnp.sqrt(result + 1e-05)
    for one in pending:
        one.wait_send()


def fused_call(tokens, cotangent, routes, probs, gate_weight, up_weight, down_weight, keep):
    planes = lax.axis_size("expert")
    count = planes * 4
    units, width = gate_weight.shape[1:]
    dma = pltpu.SemaphoreType.DMA
    vmem, hbm = pl.BlockSpec(memory_space=pltpu.VMEM), pl.BlockSpec(memory_space=pl.ANY)
    sends = 3 * planes + 3
    return pl.pallas_call(
        functools.partial(fused, planes=planes),
        out_shape=(
            jax.ShapeDtypeStruct((1, units, 4 * units), jnp.float32),
            jax.ShapeDtypeStruct((1, units), jnp.float32),
            jax.ShapeDtypeStruct(routes.shape, jnp.float32),
        ),
        in_specs=[vmem] * 4 + [hbm] * 3 + [vmem],
        out_specs=(vmem, vmem, vmem),
        scratch_shapes=[
            pltpu.VMEM((count, SLOT, LANES + width), jnp.bfloat16),
            pltpu.VMEM((count, SLOT, width), jnp.bfloat16),
            pltpu.VMEM((2 * units, width), jnp.bfloat16),
            pltpu.VMEM((units, width), jnp.bfloat16),
            pltpu.VMEM((3, count * SLOT, 2 * units // 3), jnp.float32),
            pltpu.VMEM((count * SLOT, units), jnp.float32),
            pltpu.VMEM((4, count * 12, units), jnp.bfloat16),
            pltpu.VMEM((count, SLOT, LANES), jnp.float32),
            pltpu.VMEM((planes, SLOT, LANES), jnp.float32),
            dma((3,)), dma((sends + planes,)), dma((count,)), dma((sends + planes,)), dma((count,)),
            dma((3,)), dma((4,)), dma((planes,)), dma((planes,)),
        ],
        compiler_params=pltpu.CompilerParams(
            collective_id=0, has_side_effects=True, vmem_limit_bytes=48 * 1024 * 1024
        ),
        cost_estimate=pl.CostEstimate(flops=2 * 10**9, bytes_accessed=12 * 10**6, transcendentals=10**5),
        name="fisher_masks",
    )(tokens, cotangent, routes, probs, gate_weight, up_weight, down_weight, keep)


def make_grads(w_gate, w_up, w_down):

    def compute(shards, first_row):
        rows_tok, rows_cot, rows_prob = shards
        dims = (((1,), (1,)), ((), ()))
        gate_pre = lax.dot_general(w_gate, rows_tok, dims, preferred_element_type=jnp.float32)
        up_pre = lax.dot_general(w_up, rows_tok, dims, preferred_element_type=jnp.float32)
        back_pre = lax.dot_general(w_down, rows_cot, dims, preferred_element_type=jnp.float32)
        scale = rows_prob.astype(jnp.float32)[None, :]
        return (scale * (jax.nn.silu(gate_pre) * up_pre) * back_pre).astype(jnp.bfloat16)

    return compute


def local(tokens, cotangent, routes, probs, gate_weight, up_weight, down_weight, keep):
    experts = lax.axis_size("expert")
    tok_rows, picks = routes.shape
    columns, cores = lax.axis_size("dp"), lax.axis_size("sub")
    if (experts, columns, cores, tok_rows) == (4, 2, 2, 12):
        return fused_call(
            tokens, cotangent, routes, probs, gate_weight, up_weight, down_weight, keep
        )
    capacity = max(2, 2 * tok_rows * picks // experts)
    unit_count = gate_weight.shape[1]
    pair_count = tok_rows * picks
    flat_routes = routes.reshape(pair_count)
    onehot = (flat_routes[:, None] == jnp.arange(experts, dtype=jnp.int32)[None, :]).astype(
        jnp.int32
    )
    before = jnp.cumsum(onehot, axis=0) - onehot
    slot_index = jnp.sum(onehot * before, axis=1)
    target = flat_routes * capacity + slot_index
    dispatch_map = (
        jnp.arange(experts * capacity, dtype=jnp.int32)[:, None] == target[None, :]
    ).astype(jnp.float32)
    per_token = jnp.sum(dispatch_map.reshape(experts * capacity, tok_rows, picks), axis=2).astype(
        jnp.bfloat16
    )
    tok_send = jnp.dot(per_token, tokens, preferred_element_type=jnp.float32).astype(jnp.bfloat16)
    cot_send = jnp.dot(per_token, cotangent, preferred_element_type=jnp.float32).astype(
        jnp.bfloat16
    )
    prob_send = jnp.dot(
        dispatch_map, probs.astype(jnp.float32).reshape(pair_count), precision=lax.Precision.HIGHEST
    ).astype(jnp.bfloat16)
    tok_recv, cot_recv, prob_recv = (
        lax.all_to_all(tok_send, "expert", split_axis=0, concat_axis=0, tiled=True),
        lax.all_to_all(cot_send, "expert", split_axis=0, concat_axis=0, tiled=True),
        lax.all_to_all(prob_send, "expert", split_axis=0, concat_axis=0, tiled=True),
    )
    dims = (((1,), (1,)), ((), ()))
    compute = make_grads(gate_weight[0], up_weight[0], down_weight[0])
    grads_mine = compute(
        lax.all_gather((tok_recv, cot_recv, prob_recv), ("dp", "sub"), axis=0, tiled=True),
        jnp.int32(0),
    )
    squares = jnp.sum(jnp.square(grads_mine.astype(jnp.float32)), axis=0)
    owned = lax.psum_scatter(squares, ("dp", "sub"), scatter_dimension=0, tiled=True)
    fisher_rows = lax.dot_general(
        grads_mine,
        lax.all_gather(grads_mine, ("dp", "sub"), axis=0, tiled=True),
        dims,
        preferred_element_type=jnp.float32,
    )
    first_unit = lax.axis_index(("dp", "sub")) * unit_count
    returned = lax.all_to_all(owned, "expert", split_axis=0, concat_axis=0, tiled=True)
    pair_totals = jnp.dot(dispatch_map.T, returned, precision=lax.Precision.HIGHEST)
    token_scores = jnp.sqrt(pair_totals + 1e-05).reshape(tok_rows, picks)
    kept_units = keep[0].astype(jnp.float32)
    pull = jnp.dot(fisher_rows, 1.0 - kept_units, precision=lax.Precision.HIGHEST)
    diag_block = lax.dynamic_slice_in_dim(fisher_rows, first_unit, unit_count, 1)
    diagonal_part = jnp.diagonal(diag_block)
    kept_mine = lax.dynamic_slice_in_dim(kept_units, first_unit, unit_count, 0)
    masks = kept_mine * (1.0 + pull / (diagonal_part + 1e-05))
    return (fisher_rows[None], masks[None], token_scores)


def solution(mesh):
    in_specs = (
        P(("groups", "expert", "dp", "sub"), None),
        P(("groups", "expert", "dp", "sub"), None),
        P(("groups", "expert", "dp", "sub"), None),
        P(("groups", "expert", "dp", "sub"), None),
        P("expert", ("dp", "sub"), None),
        P("expert", ("dp", "sub"), None),
        P("expert", ("dp", "sub"), None),
        P("expert", None),
    )
    out_specs = (
        P(("groups", "expert"), ("dp", "sub"), None),
        P(("groups", "expert"), ("dp", "sub")),
        P(("groups", "expert", "dp", "sub"), None),
    )
    return jax.shard_map(local, mesh=mesh, in_specs=in_specs, out_specs=out_specs, check_vma=False)
```

```python
import functools

import jax
import jax.numpy as jnp
from jax import lax
from jax.experimental import pallas as pl
from jax.experimental.pallas import tpu as pltpu
from jax.sharding import PartitionSpec as P

MESH = pl.DeviceIdType.MESH
SLOT = 16
LANES = 128


def pack(values, front):
    rows, width = values.shape
    quarter = width // 4
    last = values[:, 3 * quarter:]
    folded = [last[4 * j:4 * j + 4] for j in range(3)] + [jnp.zeros((4, quarter), values.dtype)]
    lower = jnp.concatenate([jnp.zeros((4, LANES), values.dtype)] * (front is not None) + folded, axis=1)
    upper = values if front is None else jnp.concatenate([front, values], axis=1)
    return jnp.concatenate([upper, lower], axis=0)


def column_of(line):
    n = line.shape[1]
    same = lax.broadcasted_iota(jnp.int32, (n, n), 0) == lax.broadcasted_iota(jnp.int32, (n, n), 1)
    return jnp.sum(jnp.where(same, line, jnp.zeros_like(line)), axis=1, keepdims=True)


def gather_kernel(
    tokens, cotangent, routes, probs, w_gate, w_up, w_down,
    grads, returned,
    own_tok, own_cot, own_routes, own_probs, tok, cot, wgu, wd, pre, totals,
    load_sem, block_send, block_recv, grad_send, grad_recv, tot_send, tot_recv,
    *, planes,
):
    z, x, s = lax.axis_index("expert"), lax.axis_index("dp"), lax.axis_index("sub")
    units = w_down.shape[1]
    width = tokens.shape[1]
    quarter = width // 4
    count = planes * 4
    across, twin = 1 - x, 1 - s

    barrier = pltpu.get_barrier_semaphore()
    peers = []
    for k in range(planes):
        for column in range(2):
            for core in range(2):
                if k + column + core > 0:
                    peers.append((lax.rem(z + k, planes), lax.rem(x + column, 2), lax.rem(s + core, 2)))
    for plane, column, core in peers:
        pl.semaphore_signal(
            barrier, inc=1, device_id={"expert": plane, "dp": column, "sub": core}, device_id_type=MESH
        )

    small = [
        pltpu.make_async_copy(tokens, own_tok, load_sem.at[0]),
        pltpu.make_async_copy(routes, own_routes, load_sem.at[1]),
        pltpu.make_async_copy(probs, own_probs, load_sem.at[2]),
        pltpu.make_async_copy(cotangent, own_cot, load_sem.at[3]),
    ]
    loads = [
        pltpu.make_async_copy(w_gate.at[0], wgu.at[pl.ds(0, units)], load_sem.at[4]),
        pltpu.make_async_copy(w_up.at[0], wgu.at[pl.ds(units, units)], load_sem.at[5]),
        pltpu.make_async_copy(w_down.at[0], wd, load_sem.at[6]),
    ]
    for load in small:
        load.start()
    for load in loads:
        load.start()

    def slot(plane, column, core):
        return (plane * 2 + column) * 2 + core

    mine = slot(z, x, s)
    for load in small:
        load.wait()
    picks = routes.shape[0]
    lane = lax.broadcasted_iota(jnp.int32, (routes.shape[1], LANES), 1).astype(jnp.float32)
    front = jnp.zeros(lane.shape, jnp.float32)
    for k in range(picks):
        picked = column_of(own_routes[k:k + 1, :].astype(jnp.float32))
        weight = column_of(own_probs[...].astype(jnp.float32)[k:k + 1, :])
        front = front + jnp.where(lane == picked, weight, 0.0)
    tok[mine] = pack(own_tok[...].astype(jnp.float32), front).astype(jnp.bfloat16)
    cot[mine] = pack(own_cot[...].astype(jnp.float32), None).astype(jnp.bfloat16)

    pl.semaphore_wait(barrier, len(peers))

    buffers = (tok, cot)
    sent = (LANES + 3 * quarter, 3 * quarter)
    base = (LANES, 0)

    def block(a, index, kind, target):
        part = buffers[a].at[index, :, pl.ds(0, sent[a])]
        return pltpu.make_async_remote_copy(
            src_ref=part, dst_ref=part, send_sem=block_send.at[a, kind, index],
            recv_sem=block_recv.at[a, index], device_id=target, device_id_type=MESH,
        )

    def inside(plane):
        return (plane >= 0) & (plane < planes)

    def own_z(a):
        for kind, step in ((0, 1), (1, -1)):
            @pl.when(inside(z + step))
            def _():
                block(a, mine, kind, {"expert": z + step}).start()

    def to_x(a, index):
        block(a, index, 2, {"dp": across}).start()

    def to_core(a, index):
        block(a, index, 3, {"sub": twin}).start()

    def arrive(a, index):
        block(a, index, 3, {"sub": twin}).wait_recv()

    def unfold(a, index):
        folded = buffers[a][index, :, pl.ds(base[a], 3 * quarter)].astype(jnp.float32)[12:16]
        pieces = [folded[:, j * quarter:(j + 1) * quarter] for j in range(3)]
        whole = jnp.concatenate(pieces + [jnp.zeros((4, quarter), jnp.float32)], axis=0)
        buffers[a][index, :, pl.ds(base[a] + 3 * quarter, quarter)] = whole.astype(jnp.bfloat16)

    def at_distance(d, body):
        for sign in ((-1, 1) if d else (1,)):
            @pl.when(inside(z + sign * d))
            def _():
                body(z + sign * d, sign)

    def z_in(a, d):
        def body(plane, sign):
            index = slot(plane, x, s)
            arrive(a, index)

            @pl.when(inside(z - sign))
            def _():
                block(a, index, 0, {"expert": z - sign}).start()
            to_x(a, index)
            to_core(a, index)
            unfold(a, index)
        at_distance(d, body)

    def x_in(a, d):
        def body(plane, sign):
            index = slot(plane, across, s)
            arrive(a, index)
            to_core(a, index)
            unfold(a, index)
        at_distance(d, body)

    def core_in(a, d):
        def body(plane, sign):
            for column in (x, across):
                index = slot(plane, column, twin)
                arrive(a, index)
                unfold(a, index)
        at_distance(d, body)

    dims = (((1,), (1,)), ((), ()))
    step = 2 * units // 3

    def project(part):
        left = tok[:, :, pl.ds(LANES, width)].reshape(count * SLOT, width)
        pre[part] = lax.dot_general(
            left, wgu[pl.ds(part * step, step)], dims, preferred_element_type=jnp.float32
        )

    own_z(0)
    to_x(0, mine)
    to_core(0, mine)
    own_z(1)
    to_x(1, mine)
    to_core(1, mine)
    z_in(0, 1)
    x_in(0, 0)
    z_in(1, 1)
    x_in(1, 0)
    z_in(0, 2)
    x_in(0, 1)
    core_in(0, 0)
    z_in(1, 2)
    x_in(1, 1)
    core_in(1, 0)
    z_in(0, 3)
    x_in(0, 2)
    core_in(0, 1)
    z_in(1, 3)
    x_in(1, 2)
    core_in(1, 1)
    x_in(0, 3)
    core_in(0, 2)
    loads[0].wait()
    loads[1].wait()
    core_in(0, 3)
    project(0)
    x_in(1, 3)
    core_in(1, 2)
    project(1)
    project(2)
    loads[2].wait()
    core_in(1, 3)

    back = lax.dot_general(
        cot[...].reshape(count * SLOT, width), wd[...], dims, preferred_element_type=jnp.float32
    )
    both = jnp.concatenate([pre[0], pre[1], pre[2]], axis=1)
    gate, up = both[:, :units], both[:, units:]
    front_all = tok[:, :, pl.ds(0, LANES)].reshape(count * SLOT, LANES).astype(jnp.float32)
    lane_all = lax.broadcasted_iota(jnp.int32, front_all.shape, 1)
    scale = jnp.sum(jnp.where(lane_all == z, front_all, 0.0), axis=1, keepdims=True)
    row = lax.rem(lax.broadcasted_iota(jnp.int32, scale.shape, 0), SLOT)
    scale = jnp.where(row < 12, scale, 0.0)
    silu = gate / (1.0 + jnp.exp(-gate))
    value = scale * (silu * up) * back
    own = x * 2 + s
    compact = jnp.concatenate([value[SLOT * i:SLOT * i + 12] for i in range(count)], axis=0)
    grads[own] = compact.astype(jnp.bfloat16)

    def grad_copy(index, number, target):
        return pltpu.make_async_remote_copy(
            src_ref=grads.at[index], dst_ref=grads.at[index], send_sem=grad_send.at[number],
            recv_sem=grad_recv.at[index], device_id=target, device_id_type=MESH,
        )

    far = across * 2 + s
    grad_sends = [
        grad_copy(own, 0, {"dp": across}), grad_copy(own, 1, {"sub": twin}), grad_copy(far, 2, {"sub": twin})
    ]
    grad_sends[0].start()
    grad_sends[1].start()

    rounded = value.astype(jnp.bfloat16).astype(jnp.float32)
    square = jnp.zeros((count * SLOT, LANES), jnp.float32)
    for tile in range(units // LANES):
        piece = rounded[:, tile * LANES:(tile + 1) * LANES]
        square = square + piece * piece
    totals[...] = square.reshape(count, SLOT, LANES)
    total_sends = []
    for number, (plane, column, core) in enumerate(peers):
        copy = pltpu.make_async_remote_copy(
            src_ref=totals.at[slot(plane, column, core)], dst_ref=returned.at[mine],
            send_sem=tot_send.at[number], recv_sem=tot_recv.at[mine],
            device_id={"expert": plane, "dp": column, "sub": core}, device_id_type=MESH,
        )
        copy.start()
        total_sends.append(copy)
    returned[mine] = totals[mine]

    grad_copy(far, 0, {"sub": twin}).wait_recv()
    grad_sends[2].start()

    for a in range(2):
        for kind, step_z in ((0, 1), (1, -1)):
            @pl.when(inside(z + step_z))
            def _():
                block(a, mine, kind, {"expert": z + step_z}).wait_send()
        for d in range(1, planes):
            def relayed(plane, sign):
                @pl.when(inside(z - sign))
                def _():
                    block(a, slot(plane, x, s), 0, {"expert": z - sign}).wait_send()
            at_distance(d, relayed)
        for plane in range(planes):
            block(a, slot(plane, x, s), 2, {"dp": across}).wait_send()
            block(a, slot(plane, x, s), 3, {"sub": twin}).wait_send()
            block(a, slot(plane, across, s), 3, {"sub": twin}).wait_send()
    for plane, column, core in peers:
        index = slot(plane, column, core)
        pltpu.make_async_remote_copy(
            src_ref=totals.at[mine], dst_ref=returned.at[index], send_sem=tot_send.at[0],
            recv_sem=tot_recv.at[index], device_id={"sub": twin}, device_id_type=MESH,
        ).wait_recv()
    for copy in total_sends:
        copy.wait_send()
    grad_copy(x * 2 + twin, 0, {"sub": twin}).wait_recv()
    grad_copy(across * 2 + twin, 0, {"sub": twin}).wait_recv()
    for copy in grad_sends:
        copy.wait_send()


def fisher_kernel(grads, returned, routes, keep, fisher, masks, scores, held, sems, *, planes):
    own = lax.axis_index("dp") * 2 + lax.axis_index("sub")
    parts, rows, units = grads.shape
    ours = grads[own]
    flipped = ours.T
    copies = []
    for part in range(parts):
        held[part] = jnp.dot(flipped, grads[part], preferred_element_type=jnp.float32)
        copy = pltpu.make_async_copy(
            held.at[part], fisher.at[0, :, pl.ds(part * units, units)], sems.at[part]
        )
        copy.start()
        copies.append(copy)

    kept = keep[...].astype(jnp.float32)
    pulled = jnp.zeros((rows, LANES), jnp.float32)
    for part in range(parts):
        for tile in range(units // LANES):
            first = part * units + tile * LANES
            piece = grads[part, :, pl.ds(tile * LANES, LANES)].astype(jnp.float32)
            pulled = pulled + piece * (1.0 - kept[:, first:first + LANES])
    wide = ours.astype(jnp.float32)
    pull = jnp.sum(wide * jnp.sum(pulled, axis=1, keepdims=True), axis=0, keepdims=True)
    diagonal = jnp.sum(wide * wide, axis=0, keepdims=True)
    kept_mine = jnp.zeros((1, units), jnp.float32)
    for part in range(parts):
        kept_mine = kept_mine + jnp.where(own == part, kept[:, part * units:(part + 1) * units], 0.0)
    masks[...] = kept_mine * (1.0 + pull / (diagonal + 1e-05))

    choice = routes[...]
    picks, tok_rows = choice.shape
    same = (
        lax.broadcasted_iota(jnp.int32, (tok_rows, tok_rows), 0)
        == lax.broadcasted_iota(jnp.int32, (tok_rows, tok_rows), 1)
    )
    result = jnp.zeros(choice.shape, jnp.float32)
    for plane in range(planes):
        merged = returned[4 * plane] + returned[4 * plane + 1] + returned[4 * plane + 2] + returned[4 * plane + 3]
        total = jnp.sum(merged, axis=1, keepdims=True)[:tok_rows]
        line = jnp.sum(jnp.where(same, total, 0.0), axis=0, keepdims=True)
        result = result + jnp.where(choice == plane, line, 0.0)
    scores[...] = jnp.sqrt(result + 1e-05)
    for copy in copies:
        copy.wait()


def fused(tokens, cotangent, routes, probs, gate_weight, up_weight, down_weight, keep):
    planes = lax.axis_size("expert")
    count = planes * 4
    units, width = gate_weight.shape[1:]
    tok_rows, picks = routes.shape
    dma = pltpu.SemaphoreType.DMA
    vmem, hbm = pl.BlockSpec(memory_space=pltpu.VMEM), pl.BlockSpec(memory_space=pl.ANY)
    routes, probs = routes.T, probs.T
    grads, returned = pl.pallas_call(
        functools.partial(gather_kernel, planes=planes),
        out_shape=(
            jax.ShapeDtypeStruct((4, count * 12, units), jnp.bfloat16),
            jax.ShapeDtypeStruct((count, SLOT, LANES), jnp.float32),
        ),
        in_specs=[hbm] * 7,
        out_specs=(vmem, vmem),
        scratch_shapes=[
            pltpu.VMEM((tok_rows, width), jnp.bfloat16),
            pltpu.VMEM((tok_rows, width), jnp.bfloat16),
            pltpu.VMEM((picks, tok_rows), jnp.int32),
            pltpu.VMEM((picks, tok_rows), jnp.bfloat16),
            pltpu.VMEM((count, SLOT, LANES + width), jnp.bfloat16),
            pltpu.VMEM((count, SLOT, width), jnp.bfloat16),
            pltpu.VMEM((2 * units, width), jnp.bfloat16),
            pltpu.VMEM((units, width), jnp.bfloat16),
            pltpu.VMEM((3, count * SLOT, 2 * units // 3), jnp.float32),
            pltpu.VMEM((count, SLOT, LANES), jnp.float32),
            dma((7,)), dma((2, 4, count)), dma((2, count)),
            dma((3,)), dma((4,)), dma((count,)), dma((count,)),
        ],
        compiler_params=pltpu.CompilerParams(
            collective_id=0, has_side_effects=True, vmem_limit_bytes=48 * 1024 * 1024
        ),
        cost_estimate=pl.CostEstimate(flops=2 * 10**9, bytes_accessed=12 * 10**6, transcendentals=10**5),
        name="gather_grads",
    )(tokens, cotangent, routes, probs, gate_weight, up_weight, down_weight)
    fisher, masks, scores = pl.pallas_call(
        functools.partial(fisher_kernel, planes=planes),
        out_shape=(
            jax.ShapeDtypeStruct((1, units, 4 * units), jnp.float32),
            jax.ShapeDtypeStruct((1, units), jnp.float32),
            jax.ShapeDtypeStruct(routes.shape, jnp.float32),
        ),
        in_specs=[vmem] * 4,
        out_specs=(hbm, vmem, vmem),
        scratch_shapes=[pltpu.VMEM((4, units, units), jnp.float32), dma((4,))],
        compiler_params=pltpu.CompilerParams(vmem_limit_bytes=16 * 1024 * 1024),
        cost_estimate=pl.CostEstimate(flops=3 * 10**8, bytes_accessed=3 * 10**6, transcendentals=10**3),
        name="fisher_masks",
    )(grads, returned, routes, keep)
    return fisher, masks, scores.T


def make_grads(w_gate, w_up, w_down):

    def compute(shards, first_row):
        rows_tok, rows_cot, rows_prob = shards
        dims = (((1,), (1,)), ((), ()))
        gate_pre = lax.dot_general(w_gate, rows_tok, dims, preferred_element_type=jnp.float32)
        up_pre = lax.dot_general(w_up, rows_tok, dims, preferred_element_type=jnp.float32)
        back_pre = lax.dot_general(w_down, rows_cot, dims, preferred_element_type=jnp.float32)
        scale = rows_prob.astype(jnp.float32)[None, :]
        return (scale * (jax.nn.silu(gate_pre) * up_pre) * back_pre).astype(jnp.bfloat16)

    return compute


def local(tokens, cotangent, routes, probs, gate_weight, up_weight, down_weight, keep):
    experts = lax.axis_size("expert")
    tok_rows, picks = routes.shape
    columns, cores = lax.axis_size("dp"), lax.axis_size("sub")
    if (experts, columns, cores, tok_rows) == (4, 2, 2, 12):
        return fused(tokens, cotangent, routes, probs, gate_weight, up_weight, down_weight, keep)
    capacity = max(2, 2 * tok_rows * picks // experts)
    unit_count = gate_weight.shape[1]
    pair_count = tok_rows * picks
    flat_routes = routes.reshape(pair_count)
    onehot = (flat_routes[:, None] == jnp.arange(experts, dtype=jnp.int32)[None, :]).astype(
        jnp.int32
    )
    before = jnp.cumsum(onehot, axis=0) - onehot
    slot_index = jnp.sum(onehot * before, axis=1)
    target = flat_routes * capacity + slot_index
    dispatch_map = (
        jnp.arange(experts * capacity, dtype=jnp.int32)[:, None] == target[None, :]
    ).astype(jnp.float32)
    per_token = jnp.sum(dispatch_map.reshape(experts * capacity, tok_rows, picks), axis=2).astype(
        jnp.bfloat16
    )
    tok_send = jnp.dot(per_token, tokens, preferred_element_type=jnp.float32).astype(jnp.bfloat16)
    cot_send = jnp.dot(per_token, cotangent, preferred_element_type=jnp.float32).astype(
        jnp.bfloat16
    )
    prob_send = jnp.dot(
        dispatch_map, probs.astype(jnp.float32).reshape(pair_count), precision=lax.Precision.HIGHEST
    ).astype(jnp.bfloat16)
    tok_recv, cot_recv, prob_recv = (
        lax.all_to_all(tok_send, "expert", split_axis=0, concat_axis=0, tiled=True),
        lax.all_to_all(cot_send, "expert", split_axis=0, concat_axis=0, tiled=True),
        lax.all_to_all(prob_send, "expert", split_axis=0, concat_axis=0, tiled=True),
    )
    dims = (((1,), (1,)), ((), ()))
    compute = make_grads(gate_weight[0], up_weight[0], down_weight[0])
    grads_mine = compute(
        lax.all_gather((tok_recv, cot_recv, prob_recv), ("dp", "sub"), axis=0, tiled=True),
        jnp.int32(0),
    )
    squares = jnp.sum(jnp.square(grads_mine.astype(jnp.float32)), axis=0)
    owned = lax.psum_scatter(squares, ("dp", "sub"), scatter_dimension=0, tiled=True)
    fisher_rows = lax.dot_general(
        grads_mine,
        lax.all_gather(grads_mine, ("dp", "sub"), axis=0, tiled=True),
        dims,
        preferred_element_type=jnp.float32,
    )
    first_unit = lax.axis_index(("dp", "sub")) * unit_count
    returned = lax.all_to_all(owned, "expert", split_axis=0, concat_axis=0, tiled=True)
    pair_totals = jnp.dot(dispatch_map.T, returned, precision=lax.Precision.HIGHEST)
    token_scores = jnp.sqrt(pair_totals + 1e-05).reshape(tok_rows, picks)
    kept_units = keep[0].astype(jnp.float32)
    pull = jnp.dot(fisher_rows, 1.0 - kept_units, precision=lax.Precision.HIGHEST)
    diag_block = lax.dynamic_slice_in_dim(fisher_rows, first_unit, unit_count, 1)
    diagonal_part = jnp.diagonal(diag_block)
    kept_mine = lax.dynamic_slice_in_dim(kept_units, first_unit, unit_count, 0)
    masks = kept_mine * (1.0 + pull / (diagonal_part + 1e-05))
    return (fisher_rows[None], masks[None], token_scores)


def solution(mesh):
    in_specs = (
        P(("groups", "expert", "dp", "sub"), None),
        P(("groups", "expert", "dp", "sub"), None),
        P(("groups", "expert", "dp", "sub"), None),
        P(("groups", "expert", "dp", "sub"), None),
        P("expert", ("dp", "sub"), None),
        P("expert", ("dp", "sub"), None),
        P("expert", ("dp", "sub"), None),
        P("expert", None),
    )
    out_specs = (
        P(("groups", "expert"), ("dp", "sub"), None),
        P(("groups", "expert"), ("dp", "sub")),
        P(("groups", "expert", "dp", "sub"), None),
    )
    return jax.shard_map(local, mesh=mesh, in_specs=in_specs, out_specs=out_specs, check_vma=False)
```

```python
import functools

import jax
import jax.numpy as jnp
from jax import lax
from jax.experimental import pallas as pl
from jax.experimental.pallas import tpu as pltpu
from jax.sharding import PartitionSpec as P

MESH = pl.DeviceIdType.MESH
SLOT = 16
LANES = 128


def pack(values, front):
    rows, width = values.shape
    quarter = width // 4
    last = values[:, 3 * quarter:]
    folded = [last[4 * j:4 * j + 4] for j in range(3)] + [jnp.zeros((4, quarter), values.dtype)]
    lower = jnp.concatenate([jnp.zeros((4, LANES), values.dtype)] * (front is not None) + folded, axis=1)
    upper = values if front is None else jnp.concatenate([front, values], axis=1)
    return jnp.concatenate([upper, lower], axis=0)


def column_of(line):
    n = line.shape[1]
    same = lax.broadcasted_iota(jnp.int32, (n, n), 0) == lax.broadcasted_iota(jnp.int32, (n, n), 1)
    return jnp.sum(jnp.where(same, line, jnp.zeros_like(line)), axis=1, keepdims=True)


def gather_kernel(
    tokens, cotangent, routes, probs, w_gate, w_up, w_down,
    grads, returned,
    own_tok, own_cot, own_routes, own_probs, tok, cot, wgu, wd, pre, totals,
    load_sem, block_send, block_recv, grad_send, grad_recv, tot_send, tot_recv,
    *, planes,
):
    z, x, s = lax.axis_index("expert"), lax.axis_index("dp"), lax.axis_index("sub")
    units = w_down.shape[1]
    width = tokens.shape[1]
    quarter = width // 4
    count = planes * 4
    across, twin = 1 - x, 1 - s

    barrier = pltpu.get_barrier_semaphore()
    peers = []
    for k in range(planes):
        for column in range(2):
            for core in range(2):
                if k + column + core > 0:
                    peers.append((lax.rem(z + k, planes), lax.rem(x + column, 2), lax.rem(s + core, 2)))
    for plane, column, core in peers:
        pl.semaphore_signal(
            barrier, inc=1, device_id={"expert": plane, "dp": column, "sub": core}, device_id_type=MESH
        )

    small = [
        pltpu.make_async_copy(tokens, own_tok, load_sem.at[0]),
        pltpu.make_async_copy(routes, own_routes, load_sem.at[1]),
        pltpu.make_async_copy(probs, own_probs, load_sem.at[2]),
        pltpu.make_async_copy(cotangent, own_cot, load_sem.at[3]),
    ]
    loads = [
        pltpu.make_async_copy(w_gate.at[0], wgu.at[pl.ds(0, units)], load_sem.at[4]),
        pltpu.make_async_copy(w_up.at[0], wgu.at[pl.ds(units, units)], load_sem.at[5]),
        pltpu.make_async_copy(w_down.at[0], wd, load_sem.at[6]),
    ]
    for load in small:
        load.start()
    for load in loads:
        load.start()

    def slot(plane, column, core):
        return (plane * 2 + column) * 2 + core

    mine = slot(z, x, s)
    for load in small:
        load.wait()
    picks = routes.shape[0]
    lane = lax.broadcasted_iota(jnp.int32, (routes.shape[1], LANES), 1).astype(jnp.float32)
    front = jnp.zeros(lane.shape, jnp.float32)
    for k in range(picks):
        picked = column_of(own_routes[k:k + 1, :].astype(jnp.float32))
        weight = column_of(own_probs[...].astype(jnp.float32)[k:k + 1, :])
        front = front + jnp.where(lane == picked, weight, 0.0)
    tok[mine] = pack(own_tok[...].astype(jnp.float32), front).astype(jnp.bfloat16)
    cot[mine] = pack(own_cot[...].astype(jnp.float32), None).astype(jnp.bfloat16)

    pl.semaphore_wait(barrier, len(peers))

    buffers = (tok, cot)
    sent = (LANES + 3 * quarter, 3 * quarter)
    base = (LANES, 0)

    def block(a, index, kind, target):
        part = buffers[a].at[index, :, pl.ds(0, sent[a])]
        return pltpu.make_async_remote_copy(
            src_ref=part, dst_ref=part, send_sem=block_send.at[a, kind],
            recv_sem=block_recv.at[a, index], device_id=target, device_id_type=MESH,
        )

    def inside(plane):
        return (plane >= 0) & (plane < planes)

    def own_z(a):
        for step in (1, -1):
            @pl.when(inside(z + step))
            def _():
                block(a, mine, 0, {"expert": z + step}).start()

    def to_x(a, index):
        block(a, index, 1, {"dp": across}).start()

    def to_core(a, index):
        block(a, index, 2, {"sub": twin}).start()

    def arrive(a, index):
        block(a, index, 2, {"sub": twin}).wait_recv()

    def unfold(a, index):
        folded = buffers[a][index, :, pl.ds(base[a], 3 * quarter)].astype(jnp.float32)[12:16]
        pieces = [folded[:, j * quarter:(j + 1) * quarter] for j in range(3)]
        whole = jnp.concatenate(pieces + [jnp.zeros((4, quarter), jnp.float32)], axis=0)
        buffers[a][index, :, pl.ds(base[a] + 3 * quarter, quarter)] = whole.astype(jnp.bfloat16)

    def at_distance(d, body):
        for sign in ((-1, 1) if d else (1,)):
            @pl.when(inside(z + sign * d))
            def _():
                body(z + sign * d, sign)

    def z_in(a, d):
        def body(plane, sign):
            index = slot(plane, x, s)
            arrive(a, index)

            @pl.when(inside(z - sign))
            def _():
                block(a, index, 0, {"expert": z - sign}).start()
            to_x(a, index)
            to_core(a, index)
            unfold(a, index)
        at_distance(d, body)

    def x_in(a, d):
        def body(plane, sign):
            index = slot(plane, across, s)
            arrive(a, index)
            to_core(a, index)
            unfold(a, index)
        at_distance(d, body)

    def core_in(a, d):
        def body(plane, sign):
            for column in (x, across):
                index = slot(plane, column, twin)
                arrive(a, index)
                unfold(a, index)
        at_distance(d, body)

    dims = (((1,), (1,)), ((), ()))
    step = 2 * units // 3

    def project(part):
        left = tok[:, :, pl.ds(LANES, width)].reshape(count * SLOT, width)
        pre[part] = lax.dot_general(
            left, wgu[pl.ds(part * step, step)], dims, preferred_element_type=jnp.float32
        )

    own_z(0)
    to_x(0, mine)
    to_core(0, mine)
    own_z(1)
    to_x(1, mine)
    to_core(1, mine)
    z_in(0, 1)
    x_in(0, 0)
    z_in(1, 1)
    x_in(1, 0)
    z_in(0, 2)
    x_in(0, 1)
    core_in(0, 0)
    z_in(1, 2)
    x_in(1, 1)
    core_in(1, 0)
    z_in(0, 3)
    x_in(0, 2)
    core_in(0, 1)
    z_in(1, 3)
    x_in(1, 2)
    core_in(1, 1)
    x_in(0, 3)
    core_in(0, 2)
    loads[0].wait()
    loads[1].wait()
    core_in(0, 3)
    project(0)
    x_in(1, 3)
    core_in(1, 2)
    project(1)
    project(2)
    loads[2].wait()
    core_in(1, 3)

    back = lax.dot_general(
        cot[...].reshape(count * SLOT, width), wd[...], dims, preferred_element_type=jnp.float32
    )
    both = jnp.concatenate([pre[0], pre[1], pre[2]], axis=1)
    gate, up = both[:, :units], both[:, units:]
    front_all = tok[:, :, pl.ds(0, LANES)].reshape(count * SLOT, LANES).astype(jnp.float32)
    lane_all = lax.broadcasted_iota(jnp.int32, front_all.shape, 1)
    scale = jnp.sum(jnp.where(lane_all == z, front_all, 0.0), axis=1, keepdims=True)
    row = lax.rem(lax.broadcasted_iota(jnp.int32, scale.shape, 0), SLOT)
    scale = jnp.where(row < 12, scale, 0.0)
    silu = gate / (1.0 + jnp.exp(-gate))
    value = scale * (silu * up) * back
    own = x * 2 + s
    compact = jnp.concatenate([value[SLOT * i:SLOT * i + 12] for i in range(count)], axis=0)
    grads[own] = compact.astype(jnp.bfloat16)

    def grad_copy(index, number, target):
        return pltpu.make_async_remote_copy(
            src_ref=grads.at[index], dst_ref=grads.at[index], send_sem=grad_send.at[number],
            recv_sem=grad_recv.at[index], device_id=target, device_id_type=MESH,
        )

    far = across * 2 + s
    grad_sends = [
        grad_copy(own, 0, {"dp": across}), grad_copy(own, 1, {"sub": twin}), grad_copy(far, 2, {"sub": twin})
    ]
    grad_sends[0].start()
    grad_sends[1].start()

    rounded = value.astype(jnp.bfloat16).astype(jnp.float32)
    square = jnp.zeros((count * SLOT, LANES), jnp.float32)
    for tile in range(units // LANES):
        piece = rounded[:, tile * LANES:(tile + 1) * LANES]
        square = square + piece * piece
    totals[...] = square.reshape(count, SLOT, LANES)
    for plane, column, core in peers:
        pltpu.make_async_remote_copy(
            src_ref=totals.at[slot(plane, column, core)], dst_ref=returned.at[mine],
            send_sem=tot_send, recv_sem=tot_recv,
            device_id={"expert": plane, "dp": column, "sub": core}, device_id_type=MESH,
        ).start()
    returned[mine] = totals[mine]

    grad_copy(far, 0, {"sub": twin}).wait_recv()
    grad_sends[2].start()

    def sent_all(a, kind, blocks):
        part = buffers[a].at[pl.ds(0, blocks), :, pl.ds(0, sent[a])]
        pltpu.make_async_remote_copy(
            src_ref=part, dst_ref=part, send_sem=block_send.at[a, kind],
            recv_sem=block_recv.at[a, 0], device_id={"sub": twin}, device_id_type=MESH,
        ).wait_send()

    edge = (z == 0) | (z == planes - 1)
    for a in range(2):
        @pl.when(edge)
        def _():
            sent_all(a, 0, 1)

        @pl.when(jnp.logical_not(edge))
        def _():
            sent_all(a, 0, planes + 1)
        sent_all(a, 1, planes)
        sent_all(a, 2, 2 * planes)
    others = len(peers)
    every = pltpu.make_async_remote_copy(
        src_ref=totals.at[pl.ds(0, others)], dst_ref=returned.at[pl.ds(0, others)],
        send_sem=tot_send, recv_sem=tot_recv, device_id={"sub": twin}, device_id_type=MESH,
    )
    every.wait_recv()
    every.wait_send()
    grad_copy(x * 2 + twin, 0, {"sub": twin}).wait_recv()
    grad_copy(across * 2 + twin, 0, {"sub": twin}).wait_recv()
    for copy in grad_sends:
        copy.wait_send()


def fisher_kernel(grads, returned, routes, keep, fisher, masks, scores, held, sems, *, planes):
    own = lax.axis_index("dp") * 2 + lax.axis_index("sub")
    parts, rows, units = grads.shape
    ours = grads[own]
    flipped = ours.T
    copies = []
    for part in range(parts):
        held[part] = jnp.dot(flipped, grads[part], preferred_element_type=jnp.float32)
        copy = pltpu.make_async_copy(
            held.at[part], fisher.at[0, :, pl.ds(part * units, units)], sems.at[part]
        )
        copy.start()
        copies.append(copy)

    kept = keep[...].astype(jnp.float32)
    pulled = jnp.zeros((rows, LANES), jnp.float32)
    for part in range(parts):
        for tile in range(units // LANES):
            first = part * units + tile * LANES
            piece = grads[part, :, pl.ds(tile * LANES, LANES)].astype(jnp.float32)
            pulled = pulled + piece * (1.0 - kept[:, first:first + LANES])
    wide = ours.astype(jnp.float32)
    pull = jnp.sum(wide * jnp.sum(pulled, axis=1, keepdims=True), axis=0, keepdims=True)
    diagonal = jnp.sum(wide * wide, axis=0, keepdims=True)
    kept_mine = jnp.zeros((1, units), jnp.float32)
    for part in range(parts):
        kept_mine = kept_mine + jnp.where(own == part, kept[:, part * units:(part + 1) * units], 0.0)
    masks[...] = kept_mine * (1.0 + pull / (diagonal + 1e-05))

    choice = routes[...]
    picks, tok_rows = choice.shape
    same = (
        lax.broadcasted_iota(jnp.int32, (tok_rows, tok_rows), 0)
        == lax.broadcasted_iota(jnp.int32, (tok_rows, tok_rows), 1)
    )
    result = jnp.zeros(choice.shape, jnp.float32)
    for plane in range(planes):
        merged = returned[4 * plane] + returned[4 * plane + 1] + returned[4 * plane + 2] + returned[4 * plane + 3]
        total = jnp.sum(merged, axis=1, keepdims=True)[:tok_rows]
        line = jnp.sum(jnp.where(same, total, 0.0), axis=0, keepdims=True)
        result = result + jnp.where(choice == plane, line, 0.0)
    scores[...] = jnp.sqrt(result + 1e-05)
    for copy in copies:
        copy.wait()


def fused(tokens, cotangent, routes, probs, gate_weight, up_weight, down_weight, keep):
    planes = lax.axis_size("expert")
    count = planes * 4
    units, width = gate_weight.shape[1:]
    tok_rows, picks = routes.shape
    dma = pltpu.SemaphoreType.DMA
    vmem, hbm = pl.BlockSpec(memory_space=pltpu.VMEM), pl.BlockSpec(memory_space=pl.ANY)
    routes, probs = routes.T, probs.T
    grads, returned = pl.pallas_call(
        functools.partial(gather_kernel, planes=planes),
        out_shape=(
            pltpu.VMEM((4, count * 12, units), jnp.bfloat16),
            pltpu.VMEM((count, SLOT, LANES), jnp.float32),
        ),
        in_specs=[hbm] * 7,
        out_specs=(vmem, vmem),
        scratch_shapes=[
            pltpu.VMEM((tok_rows, width), jnp.bfloat16),
            pltpu.VMEM((tok_rows, width), jnp.bfloat16),
            pltpu.VMEM((picks, tok_rows), jnp.int32),
            pltpu.VMEM((picks, tok_rows), jnp.bfloat16),
            pltpu.VMEM((count, SLOT, LANES + width), jnp.bfloat16),
            pltpu.VMEM((count, SLOT, width), jnp.bfloat16),
            pltpu.VMEM((2 * units, width), jnp.bfloat16),
            pltpu.VMEM((units, width), jnp.bfloat16),
            pltpu.VMEM((3, count * SLOT, 2 * units // 3), jnp.float32),
            pltpu.VMEM((count, SLOT, LANES), jnp.float32),
            dma((7,)), dma((2, 3)), dma((2, count)),
            dma((3,)), dma((4,)), dma, dma,
        ],
        compiler_params=pltpu.CompilerParams(
            collective_id=0, has_side_effects=True, vmem_limit_bytes=60 * 1024 * 1024
        ),
        cost_estimate=pl.CostEstimate(flops=2 * 10**9, bytes_accessed=12 * 10**6, transcendentals=10**5),
        name="gather_grads",
    )(tokens, cotangent, routes, probs, gate_weight, up_weight, down_weight)
    fisher, masks, scores = pl.pallas_call(
        functools.partial(fisher_kernel, planes=planes),
        out_shape=(
            jax.ShapeDtypeStruct((1, units, 4 * units), jnp.float32),
            jax.ShapeDtypeStruct((1, units), jnp.float32),
            jax.ShapeDtypeStruct(routes.shape, jnp.float32),
        ),
        in_specs=[vmem] * 4,
        out_specs=(hbm, vmem, vmem),
        scratch_shapes=[pltpu.VMEM((4, units, units), jnp.float32), dma((4,))],
        compiler_params=pltpu.CompilerParams(vmem_limit_bytes=16 * 1024 * 1024),
        cost_estimate=pl.CostEstimate(flops=3 * 10**8, bytes_accessed=3 * 10**6, transcendentals=10**3),
        name="fisher_masks",
    )(grads, returned, routes, keep)
    return fisher, masks, scores.T


def make_grads(w_gate, w_up, w_down):

    def compute(shards, first_row):
        rows_tok, rows_cot, rows_prob = shards
        dims = (((1,), (1,)), ((), ()))
        gate_pre = lax.dot_general(w_gate, rows_tok, dims, preferred_element_type=jnp.float32)
        up_pre = lax.dot_general(w_up, rows_tok, dims, preferred_element_type=jnp.float32)
        back_pre = lax.dot_general(w_down, rows_cot, dims, preferred_element_type=jnp.float32)
        scale = rows_prob.astype(jnp.float32)[None, :]
        return (scale * (jax.nn.silu(gate_pre) * up_pre) * back_pre).astype(jnp.bfloat16)

    return compute


def local(tokens, cotangent, routes, probs, gate_weight, up_weight, down_weight, keep):
    experts = lax.axis_size("expert")
    tok_rows, picks = routes.shape
    columns, cores = lax.axis_size("dp"), lax.axis_size("sub")
    if (experts, columns, cores, tok_rows) == (4, 2, 2, 12):
        return fused(tokens, cotangent, routes, probs, gate_weight, up_weight, down_weight, keep)
    capacity = max(2, 2 * tok_rows * picks // experts)
    unit_count = gate_weight.shape[1]
    pair_count = tok_rows * picks
    flat_routes = routes.reshape(pair_count)
    onehot = (flat_routes[:, None] == jnp.arange(experts, dtype=jnp.int32)[None, :]).astype(
        jnp.int32
    )
    before = jnp.cumsum(onehot, axis=0) - onehot
    slot_index = jnp.sum(onehot * before, axis=1)
    target = flat_routes * capacity + slot_index
    dispatch_map = (
        jnp.arange(experts * capacity, dtype=jnp.int32)[:, None] == target[None, :]
    ).astype(jnp.float32)
    per_token = jnp.sum(dispatch_map.reshape(experts * capacity, tok_rows, picks), axis=2).astype(
        jnp.bfloat16
    )
    tok_send = jnp.dot(per_token, tokens, preferred_element_type=jnp.float32).astype(jnp.bfloat16)
    cot_send = jnp.dot(per_token, cotangent, preferred_element_type=jnp.float32).astype(
        jnp.bfloat16
    )
    prob_send = jnp.dot(
        dispatch_map, probs.astype(jnp.float32).reshape(pair_count), precision=lax.Precision.HIGHEST
    ).astype(jnp.bfloat16)
    tok_recv, cot_recv, prob_recv = (
        lax.all_to_all(tok_send, "expert", split_axis=0, concat_axis=0, tiled=True),
        lax.all_to_all(cot_send, "expert", split_axis=0, concat_axis=0, tiled=True),
        lax.all_to_all(prob_send, "expert", split_axis=0, concat_axis=0, tiled=True),
    )
    dims = (((1,), (1,)), ((), ()))
    compute = make_grads(gate_weight[0], up_weight[0], down_weight[0])
    grads_mine = compute(
        lax.all_gather((tok_recv, cot_recv, prob_recv), ("dp", "sub"), axis=0, tiled=True),
        jnp.int32(0),
    )
    squares = jnp.sum(jnp.square(grads_mine.astype(jnp.float32)), axis=0)
    owned = lax.psum_scatter(squares, ("dp", "sub"), scatter_dimension=0, tiled=True)
    fisher_rows = lax.dot_general(
        grads_mine,
        lax.all_gather(grads_mine, ("dp", "sub"), axis=0, tiled=True),
        dims,
        preferred_element_type=jnp.float32,
    )
    first_unit = lax.axis_index(("dp", "sub")) * unit_count
    returned = lax.all_to_all(owned, "expert", split_axis=0, concat_axis=0, tiled=True)
    pair_totals = jnp.dot(dispatch_map.T, returned, precision=lax.Precision.HIGHEST)
    token_scores = jnp.sqrt(pair_totals + 1e-05).reshape(tok_rows, picks)
    kept_units = keep[0].astype(jnp.float32)
    pull = jnp.dot(fisher_rows, 1.0 - kept_units, precision=lax.Precision.HIGHEST)
    diag_block = lax.dynamic_slice_in_dim(fisher_rows, first_unit, unit_count, 1)
    diagonal_part = jnp.diagonal(diag_block)
    kept_mine = lax.dynamic_slice_in_dim(kept_units, first_unit, unit_count, 0)
    masks = kept_mine * (1.0 + pull / (diagonal_part + 1e-05))
    return (fisher_rows[None], masks[None], token_scores)


def solution(mesh):
    in_specs = (
        P(("groups", "expert", "dp", "sub"), None),
        P(("groups", "expert", "dp", "sub"), None),
        P(("groups", "expert", "dp", "sub"), None),
        P(("groups", "expert", "dp", "sub"), None),
        P("expert", ("dp", "sub"), None),
        P("expert", ("dp", "sub"), None),
        P("expert", ("dp", "sub"), None),
        P("expert", None),
    )
    out_specs = (
        P(("groups", "expert"), ("dp", "sub"), None),
        P(("groups", "expert"), ("dp", "sub")),
        P(("groups", "expert", "dp", "sub"), None),
    )
    return jax.shard_map(local, mesh=mesh, in_specs=in_specs, out_specs=out_specs, check_vma=False)
```

```python
import functools

import jax
import jax.numpy as jnp
from jax import lax
from jax.experimental import pallas as pl
from jax.experimental.pallas import tpu as pltpu
from jax.sharding import PartitionSpec as P

MESH = pl.DeviceIdType.MESH
SLOT = 16
LANES = 128


def pack(values, front):
    rows, width = values.shape
    quarter = width // 4
    last = values[:, 3 * quarter:]
    folded = [last[4 * j:4 * j + 4] for j in range(3)] + [jnp.zeros((4, quarter), values.dtype)]
    lower = jnp.concatenate([jnp.zeros((4, LANES), values.dtype)] * (front is not None) + folded, axis=1)
    upper = values if front is None else jnp.concatenate([front, values], axis=1)
    return jnp.concatenate([upper, lower], axis=0)


def column_of(line):
    n = line.shape[1]
    same = lax.broadcasted_iota(jnp.int32, (n, n), 0) == lax.broadcasted_iota(jnp.int32, (n, n), 1)
    return jnp.sum(jnp.where(same, line, jnp.zeros_like(line)), axis=1, keepdims=True)


def gather_kernel(
    tokens, cotangent, routes, probs, w_gate, w_up, w_down,
    grads, returned,
    own_tok, own_cot, own_routes, own_probs, tok, cot, wgu, wd, pre, totals,
    load_sem, block_send, block_recv, grad_send, grad_recv, tot_send, tot_recv,
    *, planes,
):
    z, x, s = lax.axis_index("expert"), lax.axis_index("dp"), lax.axis_index("sub")
    units = w_down.shape[1]
    width = tokens.shape[1]
    quarter = width // 4
    count = planes * 4
    across, twin = 1 - x, 1 - s

    barrier = pltpu.get_barrier_semaphore()
    peers = []
    for k in range(planes):
        for column in range(2):
            for core in range(2):
                if k + column + core > 0:
                    peers.append((lax.rem(z + k, planes), lax.rem(x + column, 2), lax.rem(s + core, 2)))
    for plane, column, core in peers:
        pl.semaphore_signal(
            barrier, inc=1, device_id={"expert": plane, "dp": column, "sub": core}, device_id_type=MESH
        )

    small = [
        pltpu.make_async_copy(tokens, own_tok, load_sem.at[0]),
        pltpu.make_async_copy(routes, own_routes, load_sem.at[1]),
        pltpu.make_async_copy(probs, own_probs, load_sem.at[2]),
        pltpu.make_async_copy(cotangent, own_cot, load_sem.at[3]),
    ]
    loads = [
        pltpu.make_async_copy(w_gate.at[0], wgu.at[pl.ds(0, units)], load_sem.at[4]),
        pltpu.make_async_copy(w_up.at[0], wgu.at[pl.ds(units, units)], load_sem.at[5]),
        pltpu.make_async_copy(w_down.at[0], wd, load_sem.at[6]),
    ]
    for load in small:
        load.start()
    for load in loads:
        load.start()

    def slot(plane, column, core):
        return (plane * 2 + column) * 2 + core

    mine = slot(z, x, s)
    for load in small:
        load.wait()
    picks = routes.shape[0]
    lane = lax.broadcasted_iota(jnp.int32, (routes.shape[1], LANES), 1).astype(jnp.float32)
    front = jnp.zeros(lane.shape, jnp.float32)
    for k in range(picks):
        picked = column_of(own_routes[k:k + 1, :].astype(jnp.float32))
        weight = column_of(own_probs[...].astype(jnp.float32)[k:k + 1, :])
        front = front + jnp.where(lane == picked, weight, 0.0)
    tok[mine] = pack(own_tok[...].astype(jnp.float32), front).astype(jnp.bfloat16)
    cot[mine] = pack(own_cot[...].astype(jnp.float32), None).astype(jnp.bfloat16)

    pl.semaphore_wait(barrier, len(peers))

    buffers = (tok, cot)
    sent = (LANES + 3 * quarter, 3 * quarter)
    base = (LANES, 0)

    def block(a, index, kind, target):
        part = buffers[a].at[index, :, pl.ds(0, sent[a])]
        return pltpu.make_async_remote_copy(
            src_ref=part, dst_ref=part, send_sem=block_send.at[a, kind],
            recv_sem=block_recv.at[a, index], device_id=target, device_id_type=MESH,
        )

    def inside(plane):
        return (plane >= 0) & (plane < planes)

    def own_z(a):
        for step in (1, -1):
            @pl.when(inside(z + step))
            def _():
                block(a, mine, 0, {"expert": z + step}).start()

    def to_x(a, index):
        block(a, index, 1, {"dp": across}).start()

    def to_core(a, index):
        block(a, index, 2, {"sub": twin}).start()

    def arrive(a, index):
        block(a, index, 2, {"sub": twin}).wait_recv()

    def unfold(a, index):
        folded = buffers[a][index, :, pl.ds(base[a], 3 * quarter)].astype(jnp.float32)[12:16]
        pieces = [folded[:, j * quarter:(j + 1) * quarter] for j in range(3)]
        whole = jnp.concatenate(pieces + [jnp.zeros((4, quarter), jnp.float32)], axis=0)
        buffers[a][index, :, pl.ds(base[a] + 3 * quarter, quarter)] = whole.astype(jnp.bfloat16)

    def at_distance(d, body):
        for sign in ((-1, 1) if d else (1,)):
            @pl.when(inside(z + sign * d))
            def _():
                body(z + sign * d, sign)

    def z_in(a, d):
        def body(plane, sign):
            index = slot(plane, x, s)
            arrive(a, index)

            @pl.when(inside(z - sign))
            def _():
                block(a, index, 0, {"expert": z - sign}).start()
            to_x(a, index)
            to_core(a, index)
            unfold(a, index)
        at_distance(d, body)

    def x_in(a, d):
        def body(plane, sign):
            index = slot(plane, across, s)
            arrive(a, index)
            to_core(a, index)
            unfold(a, index)
        at_distance(d, body)

    def core_in(a, d):
        def body(plane, sign):
            for column in (x, across):
                index = slot(plane, column, twin)
                arrive(a, index)
                unfold(a, index)
        at_distance(d, body)

    dims = (((1,), (1,)), ((), ()))
    step = 2 * units // 3

    def project(part):
        left = tok[:, :, pl.ds(LANES, width)].reshape(count * SLOT, width)
        pre[part] = lax.dot_general(
            left, wgu[pl.ds(part * step, step)], dims, preferred_element_type=jnp.float32
        )

    own_z(0)
    to_x(0, mine)
    to_core(0, mine)
    own_z(1)
    to_x(1, mine)
    to_core(1, mine)
    z_in(0, 1)
    x_in(0, 0)
    z_in(1, 1)
    x_in(1, 0)
    z_in(0, 2)
    x_in(0, 1)
    core_in(0, 0)
    z_in(1, 2)
    x_in(1, 1)
    core_in(1, 0)
    z_in(0, 3)
    x_in(0, 2)
    core_in(0, 1)
    z_in(1, 3)
    x_in(1, 2)
    core_in(1, 1)
    x_in(0, 3)
    core_in(0, 2)
    loads[0].wait()
    loads[1].wait()
    core_in(0, 3)
    x_in(1, 3)
    project(0)
    project(1)
    project(2)
    core_in(1, 2)
    loads[2].wait()
    core_in(1, 3)

    back = lax.dot_general(
        cot[...].reshape(count * SLOT, width), wd[...], dims, preferred_element_type=jnp.float32
    )
    both = jnp.concatenate([pre[0], pre[1], pre[2]], axis=1)
    gate, up = both[:, :units], both[:, units:]
    front_all = tok[:, :, pl.ds(0, LANES)].reshape(count * SLOT, LANES).astype(jnp.float32)
    lane_all = lax.broadcasted_iota(jnp.int32, front_all.shape, 1)
    scale = jnp.sum(jnp.where(lane_all == z, front_all, 0.0), axis=1, keepdims=True)
    row = lax.rem(lax.broadcasted_iota(jnp.int32, scale.shape, 0), SLOT)
    scale = jnp.where(row < 12, scale, 0.0)
    own = x * 2 + s
    far = across * 2 + s
    half = count * 6

    def grad_copy(index, piece, number, target):
        part = grads.at[index, pl.ds(piece * half, half)]
        return pltpu.make_async_remote_copy(
            src_ref=part, dst_ref=part, send_sem=grad_send.at[piece, number],
            recv_sem=grad_recv.at[piece, index], device_id=target, device_id_type=MESH,
        )

    grad_sends = []

    def grad_start(index, piece, number, target):
        copy = grad_copy(index, piece, number, target)
        copy.start()
        grad_sends.append(copy)

    halves = []
    for piece in range(2):
        rows = slice(piece * count * SLOT // 2, (piece + 1) * count * SLOT // 2)
        silu = gate[rows] / (1.0 + jnp.exp(-gate[rows]))
        value = scale[rows] * (silu * up[rows]) * back[rows]
        compact = jnp.concatenate([value[SLOT * i:SLOT * i + 12] for i in range(count // 2)], axis=0)
        grads[own, pl.ds(piece * half, half)] = compact.astype(jnp.bfloat16)
        grad_start(own, piece, 0, {"dp": across})
        grad_start(own, piece, 1, {"sub": twin})
        halves.append(value)

    rounded = jnp.concatenate(halves, axis=0).astype(jnp.bfloat16).astype(jnp.float32)
    square = jnp.zeros((count * SLOT, LANES), jnp.float32)
    for tile in range(units // LANES):
        piece = rounded[:, tile * LANES:(tile + 1) * LANES]
        square = square + piece * piece
    spread = jnp.where(
        lane_all == lax.rem(lax.broadcasted_iota(jnp.int32, square.shape, 0), SLOT),
        jnp.sum(square, axis=1, keepdims=True), 0.0,
    )
    totals[...] = jnp.sum(spread.reshape(count, SLOT, LANES), axis=1, keepdims=True)
    for plane, column, core in peers:
        pltpu.make_async_remote_copy(
            src_ref=totals.at[slot(plane, column, core)], dst_ref=returned.at[mine],
            send_sem=tot_send, recv_sem=tot_recv,
            device_id={"expert": plane, "dp": column, "sub": core}, device_id_type=MESH,
        ).start()
    returned[mine] = totals[mine]

    for piece in range(2):
        grad_copy(far, piece, 0, {"sub": twin}).wait_recv()
        grad_start(far, piece, 2, {"sub": twin})

    def sent_all(a, kind, blocks):
        part = buffers[a].at[pl.ds(0, blocks), :, pl.ds(0, sent[a])]
        pltpu.make_async_remote_copy(
            src_ref=part, dst_ref=part, send_sem=block_send.at[a, kind],
            recv_sem=block_recv.at[a, 0], device_id={"sub": twin}, device_id_type=MESH,
        ).wait_send()

    edge = (z == 0) | (z == planes - 1)
    for a in range(2):
        @pl.when(edge)
        def _():
            sent_all(a, 0, 1)

        @pl.when(jnp.logical_not(edge))
        def _():
            sent_all(a, 0, planes + 1)
        sent_all(a, 1, planes)
        sent_all(a, 2, 2 * planes)
    others = len(peers)
    every = pltpu.make_async_remote_copy(
        src_ref=totals.at[pl.ds(0, others)], dst_ref=returned.at[pl.ds(0, others)],
        send_sem=tot_send, recv_sem=tot_recv, device_id={"sub": twin}, device_id_type=MESH,
    )
    every.wait_recv()
    every.wait_send()
    for piece in range(2):
        grad_copy(x * 2 + twin, piece, 0, {"sub": twin}).wait_recv()
        grad_copy(across * 2 + twin, piece, 0, {"sub": twin}).wait_recv()
    for copy in grad_sends:
        copy.wait_send()


def fisher_kernel(grads, returned, routes, keep, fisher, masks, scores, held, sems, *, planes):
    own = lax.axis_index("dp") * 2 + lax.axis_index("sub")
    parts, rows, units = grads.shape
    ours = grads[own]
    flipped = ours.T
    copies = []
    for part in range(parts):
        held[part] = jnp.dot(flipped, grads[part], preferred_element_type=jnp.float32)
        copy = pltpu.make_async_copy(
            held.at[part], fisher.at[0, :, pl.ds(part * units, units)], sems.at[part]
        )
        copy.start()
        copies.append(copy)

    kept = keep[...].astype(jnp.float32)
    pulled = jnp.zeros((rows, LANES), jnp.float32)
    for part in range(parts):
        for tile in range(units // LANES):
            first = part * units + tile * LANES
            piece = grads[part, :, pl.ds(tile * LANES, LANES)].astype(jnp.float32)
            pulled = pulled + piece * (1.0 - kept[:, first:first + LANES])
    wide = ours.astype(jnp.float32)
    pull = jnp.sum(wide * jnp.sum(pulled, axis=1, keepdims=True), axis=0, keepdims=True)
    diagonal = jnp.sum(wide * wide, axis=0, keepdims=True)
    kept_mine = jnp.zeros((1, units), jnp.float32)
    for part in range(parts):
        kept_mine = kept_mine + jnp.where(own == part, kept[:, part * units:(part + 1) * units], 0.0)
    masks[...] = kept_mine * (1.0 + pull / (diagonal + 1e-05))

    choice = routes[...]
    picks, tok_rows = choice.shape
    result = jnp.zeros(choice.shape, jnp.float32)
    for plane in range(planes):
        line = returned[4 * plane]
        for part in range(1, 4):
            line = line + returned[4 * plane + part]
        result = result + jnp.where(choice == plane, line[:, :tok_rows], 0.0)
    scores[...] = jnp.sqrt(result + 1e-05)
    for copy in copies:
        copy.wait()


def fused(tokens, cotangent, routes, probs, gate_weight, up_weight, down_weight, keep):
    planes = lax.axis_size("expert")
    count = planes * 4
    units, width = gate_weight.shape[1:]
    tok_rows, picks = routes.shape
    dma = pltpu.SemaphoreType.DMA
    vmem, hbm = pl.BlockSpec(memory_space=pltpu.VMEM), pl.BlockSpec(memory_space=pl.ANY)
    routes, probs = routes.T, probs.T
    grads, returned = pl.pallas_call(
        functools.partial(gather_kernel, planes=planes),
        out_shape=(
            pltpu.VMEM((4, count * 12, units), jnp.bfloat16),
            pltpu.VMEM((count, 1, LANES), jnp.float32),
        ),
        in_specs=[hbm] * 7,
        out_specs=(vmem, vmem),
        scratch_shapes=[
            pltpu.VMEM((tok_rows, width), jnp.bfloat16),
            pltpu.VMEM((tok_rows, width), jnp.bfloat16),
            pltpu.VMEM((picks, tok_rows), jnp.int32),
            pltpu.VMEM((picks, tok_rows), jnp.bfloat16),
            pltpu.VMEM((count, SLOT, LANES + width), jnp.bfloat16),
            pltpu.VMEM((count, SLOT, width), jnp.bfloat16),
            pltpu.VMEM((2 * units, width), jnp.bfloat16),
            pltpu.VMEM((units, width), jnp.bfloat16),
            pltpu.VMEM((3, count * SLOT, 2 * units // 3), jnp.float32),
            pltpu.VMEM((count, 1, LANES), jnp.float32),
            dma((7,)), dma((2, 3)), dma((2, count)),
            dma((2, 3)), dma((2, 4)), dma, dma,
        ],
        compiler_params=pltpu.CompilerParams(
            collective_id=0, has_side_effects=True, vmem_limit_bytes=60 * 1024 * 1024
        ),
        cost_estimate=pl.CostEstimate(flops=2 * 10**9, bytes_accessed=12 * 10**6, transcendentals=10**5),
        name="gather_grads",
    )(tokens, cotangent, routes, probs, gate_weight, up_weight, down_weight)
    fisher, masks, scores = pl.pallas_call(
        functools.partial(fisher_kernel, planes=planes),
        out_shape=(
            jax.ShapeDtypeStruct((1, units, 4 * units), jnp.float32),
            jax.ShapeDtypeStruct((1, units), jnp.float32),
            jax.ShapeDtypeStruct(routes.shape, jnp.float32),
        ),
        in_specs=[vmem] * 4,
        out_specs=(hbm, vmem, vmem),
        scratch_shapes=[pltpu.VMEM((4, units, units), jnp.float32), dma((4,))],
        compiler_params=pltpu.CompilerParams(vmem_limit_bytes=16 * 1024 * 1024),
        cost_estimate=pl.CostEstimate(flops=3 * 10**8, bytes_accessed=3 * 10**6, transcendentals=10**3),
        name="fisher_masks",
    )(grads, returned, routes, keep)
    return fisher, masks, scores.T


def make_grads(w_gate, w_up, w_down):

    def compute(shards, first_row):
        rows_tok, rows_cot, rows_prob = shards
        dims = (((1,), (1,)), ((), ()))
        gate_pre = lax.dot_general(w_gate, rows_tok, dims, preferred_element_type=jnp.float32)
        up_pre = lax.dot_general(w_up, rows_tok, dims, preferred_element_type=jnp.float32)
        back_pre = lax.dot_general(w_down, rows_cot, dims, preferred_element_type=jnp.float32)
        scale = rows_prob.astype(jnp.float32)[None, :]
        return (scale * (jax.nn.silu(gate_pre) * up_pre) * back_pre).astype(jnp.bfloat16)

    return compute


def local(tokens, cotangent, routes, probs, gate_weight, up_weight, down_weight, keep):
    experts = lax.axis_size("expert")
    tok_rows, picks = routes.shape
    columns, cores = lax.axis_size("dp"), lax.axis_size("sub")
    if (experts, columns, cores, tok_rows) == (4, 2, 2, 12):
        return fused(tokens, cotangent, routes, probs, gate_weight, up_weight, down_weight, keep)
    capacity = max(2, 2 * tok_rows * picks // experts)
    unit_count = gate_weight.shape[1]
    pair_count = tok_rows * picks
    flat_routes = routes.reshape(pair_count)
    onehot = (flat_routes[:, None] == jnp.arange(experts, dtype=jnp.int32)[None, :]).astype(
        jnp.int32
    )
    before = jnp.cumsum(onehot, axis=0) - onehot
    slot_index = jnp.sum(onehot * before, axis=1)
    target = flat_routes * capacity + slot_index
    dispatch_map = (
        jnp.arange(experts * capacity, dtype=jnp.int32)[:, None] == target[None, :]
    ).astype(jnp.float32)
    per_token = jnp.sum(dispatch_map.reshape(experts * capacity, tok_rows, picks), axis=2).astype(
        jnp.bfloat16
    )
    tok_send = jnp.dot(per_token, tokens, preferred_element_type=jnp.float32).astype(jnp.bfloat16)
    cot_send = jnp.dot(per_token, cotangent, preferred_element_type=jnp.float32).astype(
        jnp.bfloat16
    )
    prob_send = jnp.dot(
        dispatch_map, probs.astype(jnp.float32).reshape(pair_count), precision=lax.Precision.HIGHEST
    ).astype(jnp.bfloat16)
    tok_recv, cot_recv, prob_recv = (
        lax.all_to_all(tok_send, "expert", split_axis=0, concat_axis=0, tiled=True),
        lax.all_to_all(cot_send, "expert", split_axis=0, concat_axis=0, tiled=True),
        lax.all_to_all(prob_send, "expert", split_axis=0, concat_axis=0, tiled=True),
    )
    dims = (((1,), (1,)), ((), ()))
    compute = make_grads(gate_weight[0], up_weight[0], down_weight[0])
    grads_mine = compute(
        lax.all_gather((tok_recv, cot_recv, prob_recv), ("dp", "sub"), axis=0, tiled=True),
        jnp.int32(0),
    )
    squares = jnp.sum(jnp.square(grads_mine.astype(jnp.float32)), axis=0)
    owned = lax.psum_scatter(squares, ("dp", "sub"), scatter_dimension=0, tiled=True)
    fisher_rows = lax.dot_general(
        grads_mine,
        lax.all_gather(grads_mine, ("dp", "sub"), axis=0, tiled=True),
        dims,
        preferred_element_type=jnp.float32,
    )
    first_unit = lax.axis_index(("dp", "sub")) * unit_count
    returned = lax.all_to_all(owned, "expert", split_axis=0, concat_axis=0, tiled=True)
    pair_totals = jnp.dot(dispatch_map.T, returned, precision=lax.Precision.HIGHEST)
    token_scores = jnp.sqrt(pair_totals + 1e-05).reshape(tok_rows, picks)
    kept_units = keep[0].astype(jnp.float32)
    pull = jnp.dot(fisher_rows, 1.0 - kept_units, precision=lax.Precision.HIGHEST)
    diag_block = lax.dynamic_slice_in_dim(fisher_rows, first_unit, unit_count, 1)
    diagonal_part = jnp.diagonal(diag_block)
    kept_mine = lax.dynamic_slice_in_dim(kept_units, first_unit, unit_count, 0)
    masks = kept_mine * (1.0 + pull / (diagonal_part + 1e-05))
    return (fisher_rows[None], masks[None], token_scores)


def solution(mesh):
    in_specs = (
        P(("groups", "expert", "dp", "sub"), None),
        P(("groups", "expert", "dp", "sub"), None),
        P(("groups", "expert", "dp", "sub"), None),
        P(("groups", "expert", "dp", "sub"), None),
        P("expert", ("dp", "sub"), None),
        P("expert", ("dp", "sub"), None),
        P("expert", ("dp", "sub"), None),
        P("expert", None),
    )
    out_specs = (
        P(("groups", "expert"), ("dp", "sub"), None),
        P(("groups", "expert"), ("dp", "sub")),
        P(("groups", "expert", "dp", "sub"), None),
    )
    return jax.shard_map(local, mesh=mesh, in_specs=in_specs, out_specs=out_specs, check_vma=False)
```

```python
import functools

import jax
import jax.numpy as jnp
from jax import lax
from jax.experimental import pallas as pl
from jax.experimental.pallas import tpu as pltpu
from jax.sharding import PartitionSpec as P

MESH = pl.DeviceIdType.MESH
SLOT = 16
LANES = 128


def pack(values):
    quarter = values.shape[1] // 4
    last = values[:, 3 * quarter:]
    folded = [last[4 * j:4 * j + 4] for j in range(3)] + [jnp.zeros((4, quarter), values.dtype)]
    return jnp.concatenate([values, jnp.concatenate(folded, axis=1)], axis=0)


def gather_kernel(
    tokens, cotangent, routes, probs, w_gate, w_up, w_down,
    grads, returned,
    own_tok, own_cot, own_routes, own_probs, tok, cot, wgu, wd, pre, totals, told, heard,
    load_sem, block_send, block_recv, grad_send, grad_recv, tot_send, tot_recv, prob_send, prob_recv,
    *, planes,
):
    z, x, s = lax.axis_index("expert"), lax.axis_index("dp"), lax.axis_index("sub")
    units = w_down.shape[1]
    width = tokens.shape[1]
    quarter = width // 4
    count = planes * 4
    across, twin = 1 - x, 1 - s

    barrier = pltpu.get_barrier_semaphore()
    peers = []
    for k in range(planes):
        for column in range(2):
            for core in range(2):
                if k + column + core > 0:
                    peers.append((lax.rem(z + k, planes), lax.rem(x + column, 2), lax.rem(s + core, 2)))
    for plane, column, core in peers:
        pl.semaphore_signal(
            barrier, inc=1, device_id={"expert": plane, "dp": column, "sub": core}, device_id_type=MESH
        )

    small = [
        pltpu.make_async_copy(tokens, own_tok, load_sem.at[0]),
        pltpu.make_async_copy(routes, own_routes, load_sem.at[1]),
        pltpu.make_async_copy(probs, own_probs, load_sem.at[2]),
        pltpu.make_async_copy(cotangent, own_cot, load_sem.at[3]),
    ]
    loads = [
        pltpu.make_async_copy(w_gate.at[0], wgu.at[pl.ds(0, units)], load_sem.at[4]),
        pltpu.make_async_copy(w_up.at[0], wgu.at[pl.ds(units, units)], load_sem.at[5]),
        pltpu.make_async_copy(w_down.at[0], wd, load_sem.at[6]),
    ]
    for load in small:
        load.start()
    for load in loads:
        load.start()

    def slot(plane, column, core):
        return (plane * 2 + column) * 2 + core

    mine = slot(z, x, s)
    for load in small:
        load.wait()
    chosen, weight = own_routes[...], own_probs[...].astype(jnp.float32)
    blank = jnp.zeros((1, LANES - chosen.shape[1]), jnp.float32)
    for plane in range(planes):
        line = jnp.sum(jnp.where(chosen == plane, weight, 0.0), axis=0, keepdims=True)
        told[plane] = jnp.concatenate([line, blank], axis=1)
    tok[mine] = pack(own_tok[...].astype(jnp.float32)).astype(jnp.bfloat16)
    cot[mine] = pack(own_cot[...].astype(jnp.float32)).astype(jnp.bfloat16)

    pl.semaphore_wait(barrier, len(peers))

    buffers = (tok, cot)
    sent = (3 * quarter, 3 * quarter)
    base = (0, 0)

    def block(a, index, kind, target):
        part = buffers[a].at[index, :, pl.ds(0, sent[a])]
        return pltpu.make_async_remote_copy(
            src_ref=part, dst_ref=part, send_sem=block_send.at[a, kind],
            recv_sem=block_recv.at[a, index], device_id=target, device_id_type=MESH,
        )

    def inside(plane):
        return (plane >= 0) & (plane < planes)

    def own_z(a):
        for step in (1, -1):
            @pl.when(inside(z + step))
            def _():
                block(a, mine, 0, {"expert": z + step}).start()

    def to_x(a, index):
        block(a, index, 1, {"dp": across}).start()

    def to_core(a, index):
        block(a, index, 2, {"sub": twin}).start()

    def arrive(a, index):
        block(a, index, 2, {"sub": twin}).wait_recv()

    def unfold(a, index):
        folded = buffers[a][index, :, pl.ds(base[a], 3 * quarter)].astype(jnp.float32)[12:16]
        pieces = [folded[:, j * quarter:(j + 1) * quarter] for j in range(3)]
        whole = jnp.concatenate(pieces + [jnp.zeros((4, quarter), jnp.float32)], axis=0)
        buffers[a][index, :, pl.ds(base[a] + 3 * quarter, quarter)] = whole.astype(jnp.bfloat16)

    def at_distance(d, body):
        for sign in ((-1, 1) if d else (1,)):
            @pl.when(inside(z + sign * d))
            def _():
                body(z + sign * d, sign)

    def z_in(a, d):
        def body(plane, sign):
            index = slot(plane, x, s)
            arrive(a, index)

            @pl.when(inside(z - sign))
            def _():
                block(a, index, 0, {"expert": z - sign}).start()
            to_x(a, index)
            to_core(a, index)
            unfold(a, index)
        at_distance(d, body)

    def x_in(a, d):
        def body(plane, sign):
            index = slot(plane, across, s)
            arrive(a, index)
            to_core(a, index)
            unfold(a, index)
        at_distance(d, body)

    def core_in(a, d):
        def body(plane, sign):
            for column in (x, across):
                index = slot(plane, column, twin)
                arrive(a, index)
                unfold(a, index)
        at_distance(d, body)

    dims = (((1,), (1,)), ((), ()))
    step = 2 * units // 3

    def project(part):
        left = tok[...].reshape(count * SLOT, width)
        pre[part] = lax.dot_general(
            left, wgu[pl.ds(part * step, step)], dims, preferred_element_type=jnp.float32
        )

    own_z(0)
    to_x(0, mine)
    to_core(0, mine)
    own_z(1)
    to_x(1, mine)
    to_core(1, mine)
    for plane, column, core in peers:
        pltpu.make_async_remote_copy(
            src_ref=told.at[plane], dst_ref=heard.at[mine], send_sem=prob_send, recv_sem=prob_recv,
            device_id={"expert": plane, "dp": column, "sub": core}, device_id_type=MESH,
        ).start()
    heard[mine] = told[z]
    z_in(0, 1)
    x_in(0, 0)
    z_in(1, 1)
    x_in(1, 0)
    z_in(0, 2)
    x_in(0, 1)
    core_in(0, 0)
    z_in(1, 2)
    x_in(1, 1)
    core_in(1, 0)
    z_in(0, 3)
    x_in(0, 2)
    core_in(0, 1)
    z_in(1, 3)
    x_in(1, 2)
    core_in(1, 1)
    x_in(0, 3)
    core_in(0, 2)
    loads[0].wait()
    loads[1].wait()
    core_in(0, 3)
    x_in(1, 3)
    project(0)
    project(1)
    project(2)
    core_in(1, 2)
    loads[2].wait()
    others = len(peers)
    prob_all = pltpu.make_async_remote_copy(
        src_ref=heard.at[pl.ds(0, others)], dst_ref=heard.at[pl.ds(0, others)],
        send_sem=prob_send, recv_sem=prob_recv, device_id={"sub": twin}, device_id_type=MESH,
    )
    prob_all.wait_recv()
    prob_all.wait_send()
    core_in(1, 3)

    back = lax.dot_general(
        cot[...].reshape(count * SLOT, width), wd[...], dims, preferred_element_type=jnp.float32
    )
    both = jnp.concatenate([pre[0], pre[1], pre[2]], axis=1)
    gate, up = both[:, :units], both[:, units:]
    front = jnp.broadcast_to(heard[...], (count, SLOT, LANES)).reshape(count * SLOT, LANES)
    lane_all = lax.broadcasted_iota(jnp.int32, front.shape, 1)
    at_row = lane_all == lax.rem(lax.broadcasted_iota(jnp.int32, front.shape, 0), SLOT)
    scale = jnp.sum(jnp.where(at_row, front, 0.0), axis=1, keepdims=True)
    row = lax.rem(lax.broadcasted_iota(jnp.int32, scale.shape, 0), SLOT)
    scale = jnp.where(row < 12, scale, 0.0)
    own = x * 2 + s
    far = across * 2 + s
    half = count * 6

    def grad_copy(index, piece, number, target):
        part = grads.at[index, pl.ds(piece * half, half)]
        return pltpu.make_async_remote_copy(
            src_ref=part, dst_ref=part, send_sem=grad_send.at[piece, number],
            recv_sem=grad_recv.at[piece, index], device_id=target, device_id_type=MESH,
        )

    grad_sends = []

    def grad_start(index, piece, number, target):
        copy = grad_copy(index, piece, number, target)
        copy.start()
        grad_sends.append(copy)

    halves = []
    for piece in range(2):
        rows = slice(piece * count * SLOT // 2, (piece + 1) * count * SLOT // 2)
        silu = gate[rows] / (1.0 + jnp.exp(-gate[rows]))
        value = scale[rows] * (silu * up[rows]) * back[rows]
        compact = jnp.concatenate([value[SLOT * i:SLOT * i + 12] for i in range(count // 2)], axis=0)
        grads[own, pl.ds(piece * half, half)] = compact.astype(jnp.bfloat16)
        grad_start(own, piece, 0, {"dp": across})
        grad_start(own, piece, 1, {"sub": twin})
        halves.append(value)

    rounded = jnp.concatenate(halves, axis=0).astype(jnp.bfloat16).astype(jnp.float32)
    square = jnp.zeros((count * SLOT, LANES), jnp.float32)
    for tile in range(units // LANES):
        piece = rounded[:, tile * LANES:(tile + 1) * LANES]
        square = square + piece * piece
    spread = jnp.where(at_row, jnp.sum(square, axis=1, keepdims=True), 0.0)
    totals[...] = jnp.sum(spread.reshape(count, SLOT, LANES), axis=1, keepdims=True)
    for plane, column, core in peers:
        pltpu.make_async_remote_copy(
            src_ref=totals.at[slot(plane, column, core)], dst_ref=returned.at[mine],
            send_sem=tot_send, recv_sem=tot_recv,
            device_id={"expert": plane, "dp": column, "sub": core}, device_id_type=MESH,
        ).start()
    returned[mine] = totals[mine]

    for piece in range(2):
        grad_copy(far, piece, 0, {"sub": twin}).wait_recv()
        grad_start(far, piece, 2, {"sub": twin})

    def sent_all(a, kind, blocks):
        part = buffers[a].at[pl.ds(0, blocks), :, pl.ds(0, sent[a])]
        pltpu.make_async_remote_copy(
            src_ref=part, dst_ref=part, send_sem=block_send.at[a, kind],
            recv_sem=block_recv.at[a, 0], device_id={"sub": twin}, device_id_type=MESH,
        ).wait_send()

    edge = (z == 0) | (z == planes - 1)
    for a in range(2):
        @pl.when(edge)
        def _():
            sent_all(a, 0, 1)

        @pl.when(jnp.logical_not(edge))
        def _():
            sent_all(a, 0, planes + 1)
        sent_all(a, 1, planes)
        sent_all(a, 2, 2 * planes)
    every = pltpu.make_async_remote_copy(
        src_ref=totals.at[pl.ds(0, others)], dst_ref=returned.at[pl.ds(0, others)],
        send_sem=tot_send, recv_sem=tot_recv, device_id={"sub": twin}, device_id_type=MESH,
    )
    every.wait_recv()
    every.wait_send()
    for piece in range(2):
        grad_copy(x * 2 + twin, piece, 0, {"sub": twin}).wait_recv()
        grad_copy(across * 2 + twin, piece, 0, {"sub": twin}).wait_recv()
    for copy in grad_sends:
        copy.wait_send()


def fisher_kernel(grads, returned, routes, keep, fisher, masks, scores, held, sems, *, planes):
    own = lax.axis_index("dp") * 2 + lax.axis_index("sub")
    parts, rows, units = grads.shape
    ours = grads[own]
    flipped = ours.T
    copies = []
    for part in range(parts):
        held[part] = jnp.dot(flipped, grads[part], preferred_element_type=jnp.float32)
        copy = pltpu.make_async_copy(
            held.at[part], fisher.at[0, :, pl.ds(part * units, units)], sems.at[part]
        )
        copy.start()
        copies.append(copy)

    kept = keep[...].astype(jnp.float32)
    pulled = jnp.zeros((rows, LANES), jnp.float32)
    for part in range(parts):
        for tile in range(units // LANES):
            first = part * units + tile * LANES
            piece = grads[part, :, pl.ds(tile * LANES, LANES)].astype(jnp.float32)
            pulled = pulled + piece * (1.0 - kept[:, first:first + LANES])
    wide = ours.astype(jnp.float32)
    pull = jnp.sum(wide * jnp.sum(pulled, axis=1, keepdims=True), axis=0, keepdims=True)
    diagonal = jnp.sum(wide * wide, axis=0, keepdims=True)
    kept_mine = jnp.zeros((1, units), jnp.float32)
    for part in range(parts):
        kept_mine = kept_mine + jnp.where(own == part, kept[:, part * units:(part + 1) * units], 0.0)
    masks[...] = kept_mine * (1.0 + pull / (diagonal + 1e-05))

    choice = routes[...]
    picks, tok_rows = choice.shape
    result = jnp.zeros(choice.shape, jnp.float32)
    for plane in range(planes):
        line = returned[4 * plane]
        for part in range(1, 4):
            line = line + returned[4 * plane + part]
        result = result + jnp.where(choice == plane, line[:, :tok_rows], 0.0)
    scores[...] = jnp.sqrt(result + 1e-05)
    for copy in copies:
        copy.wait()


def fused(tokens, cotangent, routes, probs, gate_weight, up_weight, down_weight, keep):
    planes = lax.axis_size("expert")
    count = planes * 4
    units, width = gate_weight.shape[1:]
    tok_rows, picks = routes.shape
    dma = pltpu.SemaphoreType.DMA
    vmem, hbm = pl.BlockSpec(memory_space=pltpu.VMEM), pl.BlockSpec(memory_space=pl.ANY)
    routes, probs = routes.T, probs.T
    grads, returned = pl.pallas_call(
        functools.partial(gather_kernel, planes=planes),
        out_shape=(
            pltpu.VMEM((4, count * 12, units), jnp.bfloat16),
            pltpu.VMEM((count, 1, LANES), jnp.float32),
        ),
        in_specs=[hbm] * 7,
        out_specs=(vmem, vmem),
        scratch_shapes=[
            pltpu.VMEM((tok_rows, width), jnp.bfloat16),
            pltpu.VMEM((tok_rows, width), jnp.bfloat16),
            pltpu.VMEM((picks, tok_rows), jnp.int32),
            pltpu.VMEM((picks, tok_rows), jnp.bfloat16),
            pltpu.VMEM((count, SLOT, width), jnp.bfloat16),
            pltpu.VMEM((count, SLOT, width), jnp.bfloat16),
            pltpu.VMEM((2 * units, width), jnp.bfloat16),
            pltpu.VMEM((units, width), jnp.bfloat16),
            pltpu.VMEM((3, count * SLOT, 2 * units // 3), jnp.float32),
            pltpu.VMEM((count, 1, LANES), jnp.float32),
            pltpu.VMEM((planes, 1, LANES), jnp.float32),
            pltpu.VMEM((count, 1, LANES), jnp.float32),
            dma((7,)), dma((2, 3)), dma((2, count)),
            dma((2, 3)), dma((2, 4)), dma, dma, dma, dma,
        ],
        compiler_params=pltpu.CompilerParams(
            collective_id=0, has_side_effects=True, vmem_limit_bytes=60 * 1024 * 1024
        ),
        cost_estimate=pl.CostEstimate(flops=2 * 10**9, bytes_accessed=12 * 10**6, transcendentals=10**5),
        name="gather_grads",
    )(tokens, cotangent, routes, probs, gate_weight, up_weight, down_weight)
    fisher, masks, scores = pl.pallas_call(
        functools.partial(fisher_kernel, planes=planes),
        out_shape=(
            jax.ShapeDtypeStruct((1, units, 4 * units), jnp.float32),
            jax.ShapeDtypeStruct((1, units), jnp.float32),
            jax.ShapeDtypeStruct(routes.shape, jnp.float32),
        ),
        in_specs=[vmem] * 4,
        out_specs=(hbm, vmem, vmem),
        scratch_shapes=[pltpu.VMEM((4, units, units), jnp.float32), dma((4,))],
        compiler_params=pltpu.CompilerParams(vmem_limit_bytes=16 * 1024 * 1024),
        cost_estimate=pl.CostEstimate(flops=3 * 10**8, bytes_accessed=3 * 10**6, transcendentals=10**3),
        name="fisher_masks",
    )(grads, returned, routes, keep)
    return fisher, masks, scores.T


def make_grads(w_gate, w_up, w_down):

    def compute(shards, first_row):
        rows_tok, rows_cot, rows_prob = shards
        dims = (((1,), (1,)), ((), ()))
        gate_pre = lax.dot_general(w_gate, rows_tok, dims, preferred_element_type=jnp.float32)
        up_pre = lax.dot_general(w_up, rows_tok, dims, preferred_element_type=jnp.float32)
        back_pre = lax.dot_general(w_down, rows_cot, dims, preferred_element_type=jnp.float32)
        scale = rows_prob.astype(jnp.float32)[None, :]
        return (scale * (jax.nn.silu(gate_pre) * up_pre) * back_pre).astype(jnp.bfloat16)

    return compute


def local(tokens, cotangent, routes, probs, gate_weight, up_weight, down_weight, keep):
    experts = lax.axis_size("expert")
    tok_rows, picks = routes.shape
    columns, cores = lax.axis_size("dp"), lax.axis_size("sub")
    if (experts, columns, cores, tok_rows) == (4, 2, 2, 12):
        return fused(tokens, cotangent, routes, probs, gate_weight, up_weight, down_weight, keep)
    capacity = max(2, 2 * tok_rows * picks // experts)
    unit_count = gate_weight.shape[1]
    pair_count = tok_rows * picks
    flat_routes = routes.reshape(pair_count)
    onehot = (flat_routes[:, None] == jnp.arange(experts, dtype=jnp.int32)[None, :]).astype(
        jnp.int32
    )
    before = jnp.cumsum(onehot, axis=0) - onehot
    slot_index = jnp.sum(onehot * before, axis=1)
    target = flat_routes * capacity + slot_index
    dispatch_map = (
        jnp.arange(experts * capacity, dtype=jnp.int32)[:, None] == target[None, :]
    ).astype(jnp.float32)
    per_token = jnp.sum(dispatch_map.reshape(experts * capacity, tok_rows, picks), axis=2).astype(
        jnp.bfloat16
    )
    tok_send = jnp.dot(per_token, tokens, preferred_element_type=jnp.float32).astype(jnp.bfloat16)
    cot_send = jnp.dot(per_token, cotangent, preferred_element_type=jnp.float32).astype(
        jnp.bfloat16
    )
    prob_send = jnp.dot(
        dispatch_map, probs.astype(jnp.float32).reshape(pair_count), precision=lax.Precision.HIGHEST
    ).astype(jnp.bfloat16)
    tok_recv, cot_recv, prob_recv = (
        lax.all_to_all(tok_send, "expert", split_axis=0, concat_axis=0, tiled=True),
        lax.all_to_all(cot_send, "expert", split_axis=0, concat_axis=0, tiled=True),
        lax.all_to_all(prob_send, "expert", split_axis=0, concat_axis=0, tiled=True),
    )
    dims = (((1,), (1,)), ((), ()))
    compute = make_grads(gate_weight[0], up_weight[0], down_weight[0])
    grads_mine = compute(
        lax.all_gather((tok_recv, cot_recv, prob_recv), ("dp", "sub"), axis=0, tiled=True),
        jnp.int32(0),
    )
    squares = jnp.sum(jnp.square(grads_mine.astype(jnp.float32)), axis=0)
    owned = lax.psum_scatter(squares, ("dp", "sub"), scatter_dimension=0, tiled=True)
    fisher_rows = lax.dot_general(
        grads_mine,
        lax.all_gather(grads_mine, ("dp", "sub"), axis=0, tiled=True),
        dims,
        preferred_element_type=jnp.float32,
    )
    first_unit = lax.axis_index(("dp", "sub")) * unit_count
    returned = lax.all_to_all(owned, "expert", split_axis=0, concat_axis=0, tiled=True)
    pair_totals = jnp.dot(dispatch_map.T, returned, precision=lax.Precision.HIGHEST)
    token_scores = jnp.sqrt(pair_totals + 1e-05).reshape(tok_rows, picks)
    kept_units = keep[0].astype(jnp.float32)
    pull = jnp.dot(fisher_rows, 1.0 - kept_units, precision=lax.Precision.HIGHEST)
    diag_block = lax.dynamic_slice_in_dim(fisher_rows, first_unit, unit_count, 1)
    diagonal_part = jnp.diagonal(diag_block)
    kept_mine = lax.dynamic_slice_in_dim(kept_units, first_unit, unit_count, 0)
    masks = kept_mine * (1.0 + pull / (diagonal_part + 1e-05))
    return (fisher_rows[None], masks[None], token_scores)


def solution(mesh):
    in_specs = (
        P(("groups", "expert", "dp", "sub"), None),
        P(("groups", "expert", "dp", "sub"), None),
        P(("groups", "expert", "dp", "sub"), None),
        P(("groups", "expert", "dp", "sub"), None),
        P("expert", ("dp", "sub"), None),
        P("expert", ("dp", "sub"), None),
        P("expert", ("dp", "sub"), None),
        P("expert", None),
    )
    out_specs = (
        P(("groups", "expert"), ("dp", "sub"), None),
        P(("groups", "expert"), ("dp", "sub")),
        P(("groups", "expert", "dp", "sub"), None),
    )
    return jax.shard_map(local, mesh=mesh, in_specs=in_specs, out_specs=out_specs, check_vma=False)
```
